32 devices in a mesh: seq: 16 (over z, x, core), head: 2 (over y).
Axes of the slice: x: 2, y: 2, z: 4, core: 2. Of those that a mesh axis runs over, the one named last changes fastest.
Arguments:
- queries: bfloat16 [12288, 2048], P(('seq', 'head')), may hold values from -6 to 6
- keys: bfloat16 [12288, 2048], P(('seq', 'head')), may hold values from -6 to 6
- values: bfloat16 [12288, 2048], P(('seq', 'head')), may hold values from -6 to 6
- out_grad: bfloat16 [12288, 2048], P(('seq', 'head')), may hold values from -6 to 6
- window: int32 [16, 2], replicated, may hold values from 0 to 1, as said below
Outputs:
- grad_queries: bfloat16 [12288, 2048], P(('seq', 'head'))
- grad_keys: bfloat16 [12288, 2048], P(('seq', 'head'))
- grad_values: bfloat16 [12288, 2048], P(('seq', 'head'))
The draws below stay inside these ranges and needn't reach their ends.
Inputs may be any that keep to these rules, and one draw needn't show every extreme that they name: `window`: some head reaches 1 along both time and height, some head 0 along both.
All inputs are finite; a program needn't handle non-finite values.
Results may differ from the reference program's by a relative error of at most 0.0066.
Values may be sent and summed in bfloat16 or wider, within the bound.
A program may use at most 192 MiB of HBM per device.

```python
import math
import jax
import jax.numpy as jnp
from jax import lax

H = 16
HD = 128
TILE = 384
GH = 4
TOKENS = 12288


def draw_queries(key, part):
    key = jax.random.fold_in(key, 1)
    noise = jnp.clip(jax.random.normal(key, (TOKENS, H * HD)), -6.0, 6.0)
    return noise.astype(jnp.bfloat16)


def draw_keys(key, part):
    key = jax.random.fold_in(key, 2)
    noise = jnp.clip(jax.random.normal(key, (TOKENS, H * HD)), -6.0, 6.0)
    return noise.astype(jnp.bfloat16)


def draw_window(key, part):
    key = jax.random.fold_in(key, 3)
    reaches = jax.random.randint(jax.random.fold_in(key, 1), (H, 2), 0, 2)
    head_order = jax.random.permutation(jax.random.fold_in(key, 2), H)
    reaches = reaches.at[head_order[0]].set(1)
    reaches = reaches.at[head_order[1]].set(0)
    return reaches.astype(jnp.int32)


def shard_levels(stream_key, extent, pieces, smallest, top_value):
    level, own = 1.0, jax.random.fold_in(stream_key, 6)
    for position, blocks in pieces:
        steps = jnp.exp(jax.random.uniform(jax.random.fold_in(own, position), (blocks,), jnp.float32, smallest / len(pieces), top_value / len(pieces)))
        level = level * jnp.repeat(steps, extent[position] // blocks).reshape([-1 if axis == position else 1 for axis in range(len(extent))])
    return level


def normal_values(key, extent, scale, limit, pieces=(), held_as=jnp.bfloat16):
    entries = jax.random.normal(key, extent, jnp.float32) * scale
    if len(pieces) > 0:
        entries = shard_levels(key, extent, pieces, -0.22, 0.18) * entries
    return jnp.clip(entries, min=-limit, max=limit).astype(held_as)


def setup_inputs(seed: int = 0) -> dict:
    arg_keys = jax.random.split(jax.random.key(seed), 6)
    return {
        "queries": draw_queries(jax.random.fold_in(arg_keys[5], 71), 0),
        "keys": draw_keys(jax.random.fold_in(arg_keys[5], 71), 0),
        "values": normal_values(arg_keys[2], (TOKENS, H * HD), 1.0, 6.0, ((0, 32),)),
        "out_grad": normal_values(arg_keys[3], (TOKENS, H * HD), 1.0, 6.0, ((0, 32),)),
        "window": draw_window(jax.random.fold_in(arg_keys[5], 71), 0),
    }


OFFSETS = tuple(((time_off, row_off) for time_off in (-1, 0, 1) for row_off in (-1, 0, 1)))

def reference(queries, keys, values, out_grad, window):
    tile_count = TOKENS // TILE
    slab_count = tile_count // 2
    grid_time = 2 * (slab_count // GH)
    score_scale = 1.0 / math.sqrt(HD)
    tile_ids = jnp.arange(tile_count, dtype=jnp.int32)
    slab_ids = tile_ids // 2
    tile_time = 2 * (slab_ids // GH) + tile_ids % 2
    tile_row = slab_ids % GH
    time_steps = jnp.array([pair[0] for pair in OFFSETS], dtype=jnp.int32)
    row_steps = jnp.array([pair[1] for pair in OFFSETS], dtype=jnp.int32)
    near_time = tile_time[:, None] + time_steps[None, :]
    near_row = tile_row[:, None] + row_steps[None, :]
    inside = (near_time >= 0) & (near_time < grid_time) & (near_row >= 0) & (near_row < GH)
    near_slab = near_time // 2 * GH + near_row
    neighbours = jnp.where(inside, 2 * near_slab + near_time % 2, 0).astype(jnp.int32)
    reach = (jnp.abs(time_steps)[None, :] <= window[:, 0:1]) & (jnp.abs(row_steps)[None, :] <= window[:, 1:2])
    tile_shape = (tile_count, TILE, H, HD)
    query_tiles = queries.reshape(tile_shape)
    key_tiles = keys.reshape(tile_shape)
    value_tiles = values.reshape(tile_shape)
    grad_tiles = out_grad.reshape(tile_shape)

    def one_tile(carry, tile_index):
        key_acc, value_acc = carry
        slots = neighbours[tile_index]
        visible = inside[tile_index][None, :] & reach
        query_here = query_tiles[tile_index].astype(jnp.float32)
        grad_here = grad_tiles[tile_index].astype(jnp.float32)
        key_near = key_tiles[slots].astype(jnp.float32)
        value_near = value_tiles[slots].astype(jnp.float32)
        scores = jnp.einsum('qnd,oknd->noqk', query_here, key_near) * score_scale
        scores = jnp.where(visible[:, :, None, None], scores, -jnp.inf)
        row_max = lax.optimization_barrier(jnp.max(scores, axis=(1, 3)))
        log_total = row_max + jnp.log(lax.optimization_barrier(jnp.sum(jnp.exp(scores - row_max[:, None, :, None]), axis=(1, 3))))
        weights = jnp.exp(scores - log_total[:, None, :, None])
        rounded = lax.optimization_barrier(weights.astype(jnp.bfloat16)).astype(jnp.float32)
        grad_scores = jnp.einsum('qnd,oknd->noqk', grad_here, value_near)
        row_delta = lax.optimization_barrier(jnp.sum(weights * grad_scores, axis=(1, 3)))
        dscore = (weights * (grad_scores - row_delta[:, None, :, None])).astype(jnp.bfloat16)
        dscore = lax.optimization_barrier(dscore).astype(jnp.float32)
        grad_query = jnp.einsum('noqk,oknd->qnd', dscore, key_near) * score_scale
        value_parts = jnp.einsum('noqk,qnd->oknd', rounded, grad_here)
        key_parts = jnp.einsum('noqk,qnd->oknd', dscore, query_here) * score_scale
        key_acc = key_acc.at[slots].add(key_parts)
        value_acc = value_acc.at[slots].add(value_parts)
        return ((key_acc, value_acc), grad_query.astype(jnp.bfloat16))
    zeros = jnp.zeros(tile_shape, jnp.float32)
    (key_acc, value_acc), grad_query = lax.scan(one_tile, (zeros, zeros), tile_ids)
    grad_queries = grad_query.reshape(TOKENS, H * HD)
    grad_keys = key_acc.astype(jnp.bfloat16).reshape(TOKENS, H * HD)
    grad_values = value_acc.astype(jnp.bfloat16).reshape(TOKENS, H * HD)
    return (grad_queries, grad_keys, grad_values)
```

```python
import functools

import jax
import jax.numpy as jnp
from jax import lax
from jax.experimental import pallas as pl
from jax.experimental.pallas import tpu as pltpu
from jax.sharding import PartitionSpec as P

HD = 128
GH = 4
SCALE = HD ** (-0.5)
LOG2E = 1.4426950408889634


def passed_along(block, axis, distance):
    devices = range(lax.axis_size(axis))
    route = [(i - distance, i) for i in devices if i - distance in devices]
    return lax.ppermute(block, axis, route)


def visible_slots(window, heads_here):
    seq_index = lax.axis_index("seq")
    grid_time = 2 * (lax.axis_size("seq") // GH)
    reaches = lax.dynamic_slice_in_dim(window, lax.axis_index("head") * heads_here, heads_here, 0)
    slot = jnp.arange(9)
    time_off, row_off = slot // 3 - 1, slot % 3 - 1
    near_time = 2 * (seq_index // GH) + jnp.arange(2)[:, None] + time_off[None, :]
    near_row = seq_index % GH + row_off
    inside = (near_time >= 0) & (near_time < grid_time)
    inside = inside & ((near_row >= 0) & (near_row < GH))[None, :]
    reach = (jnp.abs(time_off)[None, :] <= reaches[:, :1]) & (
        jnp.abs(row_off)[None, :] <= reaches[:, 1:]
    )
    return (inside[None] & reach[:, None, :]).astype(jnp.int32).reshape(-1)


def dot(a, b, dims):
    return lax.dot_general(a, b, (dims, ((), ())), preferred_element_type=jnp.float32)


def attend_kernel(
    vis_ref, q_ref, g_ref, kv_ref, dq_ref, dkv_ref, e_scr, dp_scr, acc, dqt, top, total, delta
):
    head = pl.program_id(0)
    tile = q_ref.shape[1] // 2
    acc[...] = jnp.zeros_like(acc)

    def one_tile(qt, carry):
        rows = pl.ds(pl.multiple_of(qt * tile, tile), tile)
        q = q_ref[0, rows, :]
        g = g_ref[0, rows, :]
        top[...] = jnp.full_like(top, -jnp.inf)
        total[...] = jnp.zeros_like(total)
        delta[...] = jnp.zeros_like(delta)
        dqt[...] = jnp.zeros_like(dqt)

        def over_visible(body):
            def step(slot, carry):
                @pl.when(vis_ref[(head * 2 + qt) * 9 + slot] == 1)
                def _():
                    body(slot, lax.rem(slot, 3), qt + lax.div(slot, 3))

                return carry

            lax.fori_loop(0, 9, step, 0)

        def scores(slot, row, time):
            s = dot(kv_ref[0, 0, row, time], q, ((1,), (1,)))
            top[...] = jnp.maximum(top[...], jnp.max(s, axis=0, keepdims=True))
            e_scr[slot] = s
            dp_scr[slot] = dot(kv_ref[0, 1, row, time], g, ((1,), (1,)))

        def sums(slot, row, time):
            e = jnp.exp2((e_scr[slot] - top[...]) * (SCALE * LOG2E))
            e_scr[slot] = e
            total[...] += jnp.sum(e, axis=0, keepdims=True)
            delta[...] += jnp.sum(e * dp_scr[slot], axis=0, keepdims=True)

        def grads(slot, row, time):
            p = e_scr[slot] * total[...]
            ds = (p * (dp_scr[slot] - delta[...])).astype(jnp.bfloat16)
            acc[1, row, time] += dot(p.astype(jnp.bfloat16), g, ((1,), (0,)))
            acc[0, row, time] += dot(ds, q, ((1,), (0,)))
            dqt[...] += dot(kv_ref[0, 0, row, time], ds, ((0,), (0,)))

        over_visible(scores)
        over_visible(sums)
        total[...] = 1.0 / total[...]
        delta[...] = delta[...] * total[...]
        over_visible(grads)
        dq_ref[0, rows, :] = (dqt[...] * SCALE).T.astype(jnp.bfloat16)
        return carry

    lax.fori_loop(0, 2, one_tile, 0)
    dkv_ref[0, 0] = (acc[0] * SCALE).astype(jnp.bfloat16)
    dkv_ref[0, 1] = acc[1].astype(jnp.bfloat16)


def attend(vis, q, g, kv):
    heads, rows, _ = q.shape
    tile = rows // 2
    by_head = lambda shape: pl.BlockSpec(
        (1,) + shape, lambda n, vis: (n,) + (0,) * len(shape)
    )
    pairs = heads * 18
    return pl.pallas_call(
        attend_kernel,
        grid_spec=pltpu.PrefetchScalarGridSpec(
            num_scalar_prefetch=1,
            grid=(heads,),
            in_specs=[
                by_head((rows, HD)),
                by_head((rows, HD)),
                by_head((2, 3, 4, tile, HD)),
            ],
            out_specs=[by_head((rows, HD)), by_head((2, 3, 4, tile, HD))],
            scratch_shapes=[
                pltpu.VMEM((9, tile, tile), jnp.float32),
                pltpu.VMEM((9, tile, tile), jnp.float32),
                pltpu.VMEM((2, 3, 4, tile, HD), jnp.float32),
                pltpu.VMEM((HD, tile), jnp.float32),
                pltpu.VMEM((1, tile), jnp.float32),
                pltpu.VMEM((1, tile), jnp.float32),
                pltpu.VMEM((1, tile), jnp.float32),
            ],
        ),
        out_shape=[
            jax.ShapeDtypeStruct(q.shape, jnp.bfloat16),
            jax.ShapeDtypeStruct(kv.shape, jnp.bfloat16),
        ],
        compiler_params=pltpu.CompilerParams(
            dimension_semantics=("arbitrary",), vmem_limit_bytes=48 * 2**20
        ),
        cost_estimate=pl.CostEstimate(
            flops=pairs * 5 * tile * tile * HD,
            bytes_accessed=4 * kv.size + 6 * q.size,
            transcendentals=pairs * tile * tile // 2,
        ),
        name="attend",
    )(vis, q, g, kv)


def exchange_in(queries, keys, values, out_grad):
    packed = jnp.stack([queries, keys, values, out_grad])
    here = lax.all_to_all(packed, "head", split_axis=2, concat_axis=1, tiled=True)
    rows, heads = here.shape[1], here.shape[2] // HD
    here = jnp.transpose(here.reshape(4, rows, heads, HD), (2, 0, 1, 3))
    kv = here[:, 1:3].reshape(heads, 2, 2, rows // 2, HD)
    before = passed_along(kv[:, :, 1], "seq", GH)
    after = passed_along(kv[:, :, 0], "seq", -GH)
    column = jnp.concatenate([before[:, :, None], kv, after[:, :, None]], axis=2)
    kv = jnp.stack(
        [passed_along(column, "seq", 1), column, passed_along(column, "seq", -1)], axis=2
    )
    return here[:, 0], here[:, 3], kv


def exchange_out(dq, dkv):
    column = dkv[:, :, 1].astype(jnp.float32)
    column += passed_along(dkv[:, :, 0], "seq", -1).astype(jnp.float32)
    column += passed_along(dkv[:, :, 2], "seq", 1).astype(jnp.float32)
    edges = column.astype(jnp.bfloat16)
    first = column[:, :, 1] + passed_along(edges[:, :, 3], "seq", GH).astype(jnp.float32)
    second = column[:, :, 2] + passed_along(edges[:, :, 0], "seq", -GH).astype(jnp.float32)
    own = jnp.concatenate([first, second], axis=2).astype(jnp.bfloat16)
    packed = jnp.concatenate([dq[:, None], own], axis=1)
    heads, _, rows, _ = packed.shape
    packed = jnp.transpose(packed, (1, 2, 0, 3)).reshape(3, rows, heads * HD)
    return tuple(lax.all_to_all(packed, "head", split_axis=1, concat_axis=2, tiled=True))


def per_device(queries, keys, values, out_grad, window):
    q, g, kv = exchange_in(queries, keys, values, out_grad)
    dq, dkv = attend(visible_slots(window, q.shape[0]), q, g, kv)
    return exchange_out(dq, dkv)


def solution(mesh):
    rows = P(("seq", "head"), None)
    return jax.shard_map(
        per_device,
        mesh=mesh,
        in_specs=(rows, rows, rows, rows, P()),
        out_specs=(rows, rows, rows),
        check_vma=False,
    )
```

```python
import functools

import jax
import jax.numpy as jnp
from jax import lax
from jax.experimental import pallas as pl
from jax.experimental.pallas import tpu as pltpu
from jax.sharding import PartitionSpec as P

HD = 128
GH = 4
SCALE = HD ** (-0.5)
LOG2E = 1.4426950408889634
MESH = pl.DeviceIdType.MESH


def visible_slots(window, heads_here):
    seq_index = lax.axis_index("seq")
    grid_time = 2 * (lax.axis_size("seq") // GH)
    reaches = lax.dynamic_slice_in_dim(window, lax.axis_index("head") * heads_here, heads_here, 0)
    slot = jnp.arange(9)
    time_off, row_off = slot // 3 - 1, slot % 3 - 1
    near_time = 2 * (seq_index // GH) + jnp.arange(2)[:, None] + time_off[None, :]
    near_row = seq_index % GH + row_off
    inside = (near_time >= 0) & (near_time < grid_time)
    inside = inside & ((near_row >= 0) & (near_row < GH))[None, :]
    reach = (jnp.abs(time_off)[None, :] <= reaches[:, :1]) & (
        jnp.abs(row_off)[None, :] <= reaches[:, 1:]
    )
    return (inside[None] & reach[:, None, :]).astype(jnp.int32).reshape(-1)


def dot(a, b, dims):
    return lax.dot_general(a, b, (dims, ((), ())), preferred_element_type=jnp.float32)


def attend_kernel(
    vis_ref, q_ref, g_ref, kv_ref, dq_ref, dkv_ref, e_scr, dp_scr, acc, dqt, top, total, delta
):
    head = pl.program_id(0)
    tile = q_ref.shape[1] // 2
    acc[...] = jnp.zeros_like(acc)

    def one_tile(qt, carry):
        rows = pl.ds(pl.multiple_of(qt * tile, tile), tile)
        q = q_ref[0, rows, :]
        g = g_ref[0, rows, :]
        top[...] = jnp.full_like(top, -jnp.inf)
        total[...] = jnp.zeros_like(total)
        delta[...] = jnp.zeros_like(delta)
        dqt[...] = jnp.zeros_like(dqt)

        def over_visible(body):
            def step(slot, carry):
                @pl.when(vis_ref[(head * 2 + qt) * 9 + slot] == 1)
                def _():
                    body(slot, lax.rem(slot, 3), qt + lax.div(slot, 3))

                return carry

            lax.fori_loop(0, 9, step, 0)

        def scores(slot, row, time):
            s = dot(kv_ref[0, 0, row, time], q, ((1,), (1,)))
            top[...] = jnp.maximum(top[...], jnp.max(s, axis=0, keepdims=True))
            e_scr[slot] = s
            dp_scr[slot] = dot(kv_ref[0, 1, row, time], g, ((1,), (1,)))

        def sums(slot, row, time):
            e = jnp.exp2((e_scr[slot] - top[...]) * (SCALE * LOG2E))
            e_scr[slot] = e
            total[...] += jnp.sum(e, axis=0, keepdims=True)
            delta[...] += jnp.sum(e * dp_scr[slot], axis=0, keepdims=True)

        def grads(slot, row, time):
            p = e_scr[slot] * total[...]
            ds = (p * (dp_scr[slot] - delta[...])).astype(jnp.bfloat16)
            acc[1, row, time] += dot(p.astype(jnp.bfloat16), g, ((1,), (0,)))
            acc[0, row, time] += dot(ds, q, ((1,), (0,)))
            dqt[...] += dot(kv_ref[0, 0, row, time], ds, ((0,), (0,)))

        over_visible(scores)
        over_visible(sums)
        total[...] = 1.0 / total[...]
        delta[...] = delta[...] * total[...]
        over_visible(grads)
        dq_ref[0, rows, :] = (dqt[...] * SCALE).T.astype(jnp.bfloat16)
        return carry

    lax.fori_loop(0, 2, one_tile, 0)
    dkv_ref[0, 0] = (acc[0] * SCALE).astype(jnp.bfloat16)
    dkv_ref[0, 1] = acc[1].astype(jnp.bfloat16)


def attend(vis, q, g, kv):
    heads, rows, _ = q.shape
    tile = rows // 2
    by_head = lambda shape: pl.BlockSpec(
        (1,) + shape, lambda n, vis: (n,) + (0,) * len(shape)
    )
    pairs = heads * 18
    return pl.pallas_call(
        attend_kernel,
        grid_spec=pltpu.PrefetchScalarGridSpec(
            num_scalar_prefetch=1,
            grid=(heads,),
            in_specs=[
                by_head((rows, HD)),
                by_head((rows, HD)),
                by_head((2, 3, 4, tile, HD)),
            ],
            out_specs=[by_head((rows, HD)), by_head((2, 3, 4, tile, HD))],
            scratch_shapes=[
                pltpu.VMEM((9, tile, tile), jnp.float32),
                pltpu.VMEM((9, tile, tile), jnp.float32),
                pltpu.VMEM((2, 3, 4, tile, HD), jnp.float32),
                pltpu.VMEM((HD, tile), jnp.float32),
                pltpu.VMEM((1, tile), jnp.float32),
                pltpu.VMEM((1, tile), jnp.float32),
                pltpu.VMEM((1, tile), jnp.float32),
            ],
        ),
        out_shape=[
            jax.ShapeDtypeStruct(q.shape, jnp.bfloat16),
            jax.ShapeDtypeStruct(kv.shape, jnp.bfloat16),
        ],
        compiler_params=pltpu.CompilerParams(
            dimension_semantics=("arbitrary",), vmem_limit_bytes=48 * 2**20
        ),
        cost_estimate=pl.CostEstimate(
            flops=pairs * 5 * tile * tile * HD,
            bytes_accessed=4 * kv.size + 6 * q.size,
            transcendentals=pairs * tile * tile // 2,
        ),
        name="attend",
    )(vis, q, g, kv)


def neighbours():
    seq = lax.axis_index("seq")
    row, slab = lax.rem(seq, GH), lax.div(seq, GH)
    slabs = lax.axis_size("seq") // GH
    return (
        (row > 0, seq - 1),
        (row < GH - 1, seq + 1),
        (slab > 0, seq - GH),
        (slab < slabs - 1, seq + GH),
    )


def greet(partners, peers):
    barrier = pltpu.get_barrier_semaphore()
    for peer in peers:
        pl.semaphore_signal(barrier, inc=1, device_id={"head": peer}, device_id_type=MESH)
    for exists, seq in partners:

        @pl.when(exists)
        def _():
            pl.semaphore_signal(barrier, inc=1, device_id={"seq": seq}, device_id_type=MESH)

    count = sum(exists.astype(jnp.int32) for exists, _ in partners)
    pl.semaphore_wait(barrier, count + len(peers))


def remote(src, dst, sems, index, device):
    return pltpu.make_async_remote_copy(
        src_ref=src,
        dst_ref=dst,
        send_sem=sems[0].at[index],
        recv_sem=sems[1].at[index],
        device_id=device,
        device_id_type=MESH,
    )


def for_heads(heads, body):
    def step(n, carry):
        body(n)
        return carry

    lax.fori_loop(0, heads, step, 0)


def gather_kernel(
    nh, q_in, k_in, v_in, g_in, q_out, g_out, kv_out, own, swap_s, swap_r, near_s, near_r
):
    heads, _, _, _, tile, _ = kv_out.shape
    rows = q_in.shape[0]
    h = lax.axis_index("head")
    partners = neighbours()
    up, down, before, after = partners
    peers = [lax.rem(h + j, nh) for j in range(1, nh)]
    senders = [lax.rem(h + nh - j, nh) for j in range(1, nh)]
    sources = (k_in, v_in, q_in, g_in)
    share = nh // 2

    def place(array, n, owner):
        if array < 2:
            offset = pl.multiple_of(lax.rem(owner, share) * rows, rows)
            return kv_out.at[n, array, 1, 1 + lax.div(owner, share), pl.ds(offset, rows)]
        out = q_out if array == 2 else g_out
        return out.at[n, pl.ds(pl.multiple_of(owner * rows, rows), rows)]

    def columns(array, n, owner):
        start = pl.multiple_of((owner * heads + n) * HD, HD)
        return sources[array].at[:, pl.ds(start, HD)]

    def kept(array, n):
        return pltpu.make_async_copy(columns(array, n, h), place(array, n, h), own.at[array, n])

    def swapped(array, n, j, owner):
        return remote(
            columns(array, n, peers[j]),
            place(array, n, owner),
            (swap_s, swap_r),
            (array, j, n),
            {"head": peers[j]},
        )

    def start_swap(arrays, n):
        for array in arrays:
            for j in range(nh - 1):
                swapped(array, n, j, h).start()
            kept(array, n).start()

    def wait_swap(arrays, n):
        for array in arrays:
            for j in range(nh - 1):
                swapped(array, n, j, senders[j]).wait_recv()
            kept(array, n).wait()

    def block(n, row, first, count):
        return kv_out.at[n, :, row, pl.ds(first, count)]

    def copies(kind, n):
        if kind == 0:
            mine, plan = (1, 1, 2), ((up, (2, 1, 2), (0, 1, 2)), (down, (0, 1, 2), (2, 1, 2)))
        elif kind == 1:
            plan = ((before, (1, 3, 1), (1, 0, 1)), (after, (1, 0, 1), (1, 3, 1)))
        else:
            time = 0 if kind == 2 else 3
            plan = ((up, (2, time, 1), (0, time, 1)), (down, (0, time, 1), (2, time, 1)))
        found = []
        for side, (partner, there, here) in enumerate(plan):
            if kind == 1:
                mine = (1, 1 + side, 1)
            elif kind > 1:
                mine = (1, time, 1)
            device = {"seq": partner[1]}
            send = functools.partial(
                remote,
                block(n, *mine), block(n, *there), (near_s, near_r), (kind, side, n), device
            )
            arrive = functools.partial(
                remote,
                block(n, *mine), block(n, *here), (near_s, near_r), (kind, 1 - side, n), device
            )
            found.append((partner[0], send, arrive))
        return found

    def each(kind, n, act):
        for exists, send, arrive in copies(kind, n):

            @pl.when(exists)
            def _():
                act(send, arrive)

    def start(send, arrive):
        send().start()

    greet(partners, peers)
    for_heads(heads, lambda n: start_swap((0, 1), n))

    def forward(n):
        for exists_side, kind in ((0, 2), (1, 3)):
            exists, _, arrive = copies(1, n)[exists_side]

            @pl.when(exists)
            def _():
                arrive().wait_recv()
                each(kind, n, start)

    def stage(n):
        wait_swap((0, 1), n)
        each(0, n, start)
        each(1, n, start)
        start_swap((2, 3), n)

        @pl.when(n > 0)
        def _():
            forward(n - 1)

    for_heads(heads, stage)
    forward(heads - 1)

    def finish(n):
        wait_swap((2, 3), n)
        for array in range(4):
            for j in range(nh - 1):
                swapped(array, n, j, h).wait_send()
        each(0, n, lambda send, arrive: (send().wait_send(), arrive().wait_recv()))
        each(1, n, lambda send, arrive: send().wait_send())
        for partner, kind in ((before, 2), (after, 3)):

            @pl.when(partner[0])
            def _():
                each(kind, n, lambda send, arrive: (send().wait_send(), arrive().wait_recv()))

    for_heads(heads, finish)


def exchange_in(queries, keys, values, out_grad):
    nh = lax.axis_size("head")
    rows, width = queries.shape
    heads, tile = width // HD // nh, rows * nh // 2
    dma = pltpu.SemaphoreType.DMA
    return pl.pallas_call(
        functools.partial(gather_kernel, nh),
        in_specs=[pl.BlockSpec(memory_space=pl.ANY)] * 4,
        out_specs=[pl.BlockSpec(memory_space=pl.ANY)] * 3,
        out_shape=[
            jax.ShapeDtypeStruct((heads, 2 * tile, HD), jnp.bfloat16),
            jax.ShapeDtypeStruct((heads, 2 * tile, HD), jnp.bfloat16),
            jax.ShapeDtypeStruct((heads, 2, 3, 4, tile, HD), jnp.bfloat16),
        ],
        scratch_shapes=[
            dma((4, heads)),
            dma((4, nh - 1, heads)),
            dma((4, nh - 1, heads)),
            dma((4, 2, heads)),
            dma((4, 2, heads)),
        ],
        compiler_params=pltpu.CompilerParams(collective_id=0, has_side_effects=True),
        name="gather",
    )(queries, keys, values, out_grad)


def scatter_kernel(
    nh,
    dq_in,
    dkv_in,
    dq_out,
    dk_out,
    dv_out,
    mine,
    sides,
    edges,
    times,
    final,
    load,
    own,
    swap_s,
    swap_r,
    near_s,
    near_r,
):
    heads, _, _, _, tile, _ = dkv_in.shape
    rows = dq_out.shape[0]
    h = lax.axis_index("head")
    partners = neighbours()
    up, down, before, after = partners
    peers = [lax.rem(h + j, nh) for j in range(1, nh)]
    senders = [lax.rem(h + nh - j, nh) for j in range(1, nh)]
    outs = (dk_out, dv_out, dq_out)

    def part(array, n, owner):
        span = pl.ds(pl.multiple_of(owner * rows, rows), rows)
        return dq_in.at[n, span] if array == 2 else final.at[n, array, span]

    def columns(array, n, owner):
        start = pl.multiple_of((owner * heads + n) * HD, HD)
        return outs[array].at[:, pl.ds(start, HD)]

    def kept(array, n):
        return pltpu.make_async_copy(part(array, n, h), columns(array, n, h), own.at[array, n])

    def swapped(array, n, j, owner):
        return remote(
            part(array, n, peers[j]),
            columns(array, n, owner),
            (swap_s, swap_r),
            (array, j, n),
            {"head": peers[j]},
        )

    def start_swap(arrays, n):
        for array in arrays:
            for j in range(nh - 1):
                swapped(array, n, j, h).start()
            kept(array, n).start()

    def copies(kind, n):
        if kind == 0:
            plan = ((up, 0), (down, 1))
        else:
            plan = ((before, 0), (after, 1))
        found = []
        for partner, side in plan:
            if kind == 0:
                src, dst, here = dkv_in.at[n, :, 2 * side], sides.at[n, 1 - side], sides.at[n, side]
            else:
                src, dst, here = edges.at[n, side], times.at[n, 1 - side], times.at[n, side]
            device = {"seq": partner[1]}
            send = functools.partial(
                remote, src, dst, (near_s, near_r), (kind, side, n), device)
            arrive = functools.partial(
                remote, src, here, (near_s, near_r), (kind, 1 - side, n), device)
            found.append((partner[0], send, arrive))
        return found

    def each(kind, n, act):
        for exists, send, arrive in copies(kind, n):

            @pl.when(exists)
            def _():
                act(send, arrive)

    def loaded(n):
        return pltpu.make_async_copy(dkv_in.at[n, :, 1], mine.at[n], load.at[n])

    greet(partners, peers)

    def begin(n):
        each(0, n, lambda send, arrive: send().start())
        loaded(n).start()

    for_heads(heads, begin)
    for_heads(heads, lambda n: start_swap((2,), n))
    for buffer, pair in ((sides, (up, down)), (times, (before, after))):
        for side, partner in enumerate(pair):

            @pl.when(jnp.logical_not(partner[0]))
            def _():
                def clear(n):
                    buffer[n, side] = jnp.zeros(buffer.shape[2:], buffer.dtype)

                for_heads(heads, clear)

    def column(n, which, time):
        terms = (mine[n, which, time], sides[n, 0, which, time], sides[n, 1, which, time])
        first, second, third = (term.astype(jnp.float32) for term in terms)
        return first + second + third

    def wrap_up(n):
        each(1, n, lambda send, arrive: arrive().wait_recv())
        for which in range(2):
            for place in range(2):
                total = column(n, which, 1 + place) + times[n, place, which].astype(jnp.float32)
                final[n, which, pl.ds(place * tile, tile)] = total.astype(jnp.bfloat16)
        start_swap((0, 1), n)

    def stage(n):
        each(0, n, lambda send, arrive: arrive().wait_recv())
        loaded(n).wait()
        for which in range(2):
            for side in range(2):
                edges[n, side, which] = column(n, which, 3 * side).astype(jnp.bfloat16)
        each(1, n, lambda send, arrive: send().start())

        @pl.when(n > 0)
        def _():
            wrap_up(n - 1)

    for_heads(heads, stage)
    wrap_up(heads - 1)

    def finish(n):
        for array in range(3):
            for j in range(nh - 1):
                swapped(array, n, j, h).wait_send()
                swapped(array, n, j, senders[j]).wait_recv()
            kept(array, n).wait()
        each(0, n, lambda send, arrive: send().wait_send())
        each(1, n, lambda send, arrive: send().wait_send())

    for_heads(heads, finish)


def exchange_out(dq, dkv):
    nh = lax.axis_size("head")
    heads, rows, _ = dq.shape
    tile = rows // 2
    dma = pltpu.SemaphoreType.DMA
    whole = jax.ShapeDtypeStruct((rows // nh, nh * heads * HD), jnp.bfloat16)

    def held(*shape):
        return pltpu.VMEM(shape + (HD,), jnp.bfloat16)

    return pl.pallas_call(
        functools.partial(scatter_kernel, nh),
        in_specs=[pl.BlockSpec(memory_space=pl.ANY)] * 2,
        out_specs=[pl.BlockSpec(memory_space=pl.ANY)] * 3,
        out_shape=[whole] * 3,
        scratch_shapes=[
            held(heads, 2, 4, tile),
            held(heads, 2, 2, 4, tile),
            held(heads, 2, 2, tile),
            held(heads, 2, 2, tile),
            held(heads, 2, 2 * tile),
            dma((heads,)),
            dma((3, heads)),
            dma((3, nh - 1, heads)),
            dma((3, nh - 1, heads)),
            dma((2, 2, heads)),
            dma((2, 2, heads)),
        ],
        compiler_params=pltpu.CompilerParams(
            collective_id=1, has_side_effects=True, vmem_limit_bytes=44 * 2**20
        ),
        name="scatter",
    )(dq, dkv)


def per_device(queries, keys, values, out_grad, window):
    q, g, kv = exchange_in(queries, keys, values, out_grad)
    dq, dkv = attend(visible_slots(window, q.shape[0]), q, g, kv)
    return exchange_out(dq, dkv)


def solution(mesh):
    rows = P(("seq", "head"), None)
    return jax.shard_map(
        per_device,
        mesh=mesh,
        in_specs=(rows, rows, rows, rows, P()),
        out_specs=(rows, rows, rows),
        check_vma=False,
    )
```

```python
import functools

import jax
import jax.numpy as jnp
from jax import lax
from jax.experimental import pallas as pl
from jax.experimental.pallas import tpu as pltpu
from jax.sharding import PartitionSpec as P

HD = 128
GH = 4
SCALE = HD ** (-0.5)
LOG2E = 1.4426950408889634
MESH = pl.DeviceIdType.MESH


def visible_slots(window, heads_here):
    seq_index = lax.axis_index("seq")
    grid_time = 2 * (lax.axis_size("seq") // GH)
    reaches = lax.dynamic_slice_in_dim(window, lax.axis_index("head") * heads_here, heads_here, 0)
    slot = jnp.arange(9)
    time_off, row_off = slot // 3 - 1, slot % 3 - 1
    near_time = 2 * (seq_index // GH) + jnp.arange(2)[:, None] + time_off[None, :]
    near_row = seq_index % GH + row_off
    inside = (near_time >= 0) & (near_time < grid_time)
    inside = inside & ((near_row >= 0) & (near_row < GH))[None, :]
    reach = (jnp.abs(time_off)[None, :] <= reaches[:, :1]) & (
        jnp.abs(row_off)[None, :] <= reaches[:, 1:]
    )
    return (inside[None] & reach[:, None, :]).astype(jnp.int32).reshape(-1)


def dot(a, b, dims):
    return lax.dot_general(a, b, (dims, ((), ())), preferred_element_type=jnp.float32)


def attend_kernel(
    vis_ref, q_ref, g_ref, kv_ref, dq_ref, dkv_ref, e_scr, dp_scr, acc, dqt, tops, top, total, delta
):
    head = pl.program_id(0)
    tile = q_ref.shape[1] // 2

    def seen(qt, row, time):
        step = time - qt
        inside = jnp.logical_and(step >= 0, step < 3)
        slot = jnp.clip(step, 0, 2) * 3 + row
        return jnp.logical_and(inside, vis_ref[(head * 2 + qt) * 9 + slot] == 1)

    def one_tile(qt, carry):
        rows = pl.ds(pl.multiple_of(qt * tile, tile), tile)
        q = q_ref[0, rows, :]
        g = g_ref[0, rows, :]
        top[...] = jnp.full_like(top, -jnp.inf)
        total[...] = jnp.zeros_like(total)
        delta[...] = jnp.zeros_like(delta)
        dqt[...] = jnp.zeros_like(dqt)

        def over_visible(body):
            def step(slot, carry):
                @pl.when(vis_ref[(head * 2 + qt) * 9 + slot] == 1)
                def _():
                    body(slot, lax.rem(slot, 3), qt + lax.div(slot, 3))

                return carry

            lax.fori_loop(0, 9, step, 0)

        def scores(slot, row, time):
            s = dot(kv_ref[0, 0, row, time], q, ((1,), (1,)))
            old = top[...]
            new = jnp.maximum(old, jnp.max(s, axis=0, keepdims=True))
            shrink = jnp.exp2((old - new) * (SCALE * LOG2E))
            dp = dot(kv_ref[0, 1, row, time], g, ((1,), (1,)))
            e = jnp.exp2((s - new) * (SCALE * LOG2E))
            e_scr[slot] = e
            dp_scr[slot] = dp
            tops[slot] = new
            top[...] = new
            total[...] = total[...] * shrink + jnp.sum(e, axis=0, keepdims=True)
            delta[...] = delta[...] * shrink + jnp.sum(e * dp, axis=0, keepdims=True)

        def grads(slot, row, time):
            @pl.when(jnp.logical_or(qt == 0, jnp.logical_not(seen(0, row, time))))
            def _():
                acc[:, row, time] = jnp.zeros((2,) + acc.shape[3:], jnp.float32)

            p = e_scr[slot] * (jnp.exp2((tops[slot] - top[...]) * (SCALE * LOG2E)) * total[...])
            ds = (p * (dp_scr[slot] - delta[...])).astype(jnp.bfloat16)
            acc[1, row, time] += dot(p.astype(jnp.bfloat16), g, ((1,), (0,)))
            acc[0, row, time] += dot(ds, q, ((1,), (0,)))
            dqt[...] += dot(kv_ref[0, 0, row, time], ds, ((0,), (0,)))

        over_visible(scores)
        total[...] = 1.0 / total[...]
        delta[...] = delta[...] * total[...]
        over_visible(grads)
        dq_ref[0, rows, :] = (dqt[...] * SCALE).T.astype(jnp.bfloat16)
        return carry

    lax.fori_loop(0, 2, one_tile, 0)

    def hand_out(index, carry):
        row, time = lax.div(index, 4), lax.rem(index, 4)
        used = jnp.logical_or(seen(0, row, time), seen(1, row, time))

        @pl.when(used)
        def _():
            dkv_ref[0, 0, row, time] = (acc[0, row, time] * SCALE).astype(jnp.bfloat16)
            dkv_ref[0, 1, row, time] = acc[1, row, time].astype(jnp.bfloat16)

        @pl.when(jnp.logical_not(used))
        def _():
            dkv_ref[0, :, row, time] = jnp.zeros((2,) + acc.shape[3:], jnp.bfloat16)

        return carry

    lax.fori_loop(0, 12, hand_out, 0)


def attend(vis, q, g, kv):
    heads, rows, _ = q.shape
    tile = rows // 2
    by_head = lambda shape: pl.BlockSpec(
        (1,) + shape, lambda n, vis: (n,) + (0,) * len(shape)
    )
    pairs = heads * 18
    return pl.pallas_call(
        attend_kernel,
        grid_spec=pltpu.PrefetchScalarGridSpec(
            num_scalar_prefetch=1,
            grid=(heads,),
            in_specs=[
                by_head((rows, HD)),
                by_head((rows, HD)),
                by_head((2, 3, 4, tile, HD)),
            ],
            out_specs=[by_head((rows, HD)), by_head((2, 3, 4, tile, HD))],
            scratch_shapes=[
                pltpu.VMEM((9, tile, tile), jnp.float32),
                pltpu.VMEM((9, tile, tile), jnp.float32),
                pltpu.VMEM((2, 3, 4, tile, HD), jnp.float32),
                pltpu.VMEM((HD, tile), jnp.float32),
                pltpu.VMEM((9, 1, tile), jnp.float32),
                pltpu.VMEM((1, tile), jnp.float32),
                pltpu.VMEM((1, tile), jnp.float32),
                pltpu.VMEM((1, tile), jnp.float32),
            ],
        ),
        out_shape=[
            jax.ShapeDtypeStruct(q.shape, jnp.bfloat16),
            jax.ShapeDtypeStruct(kv.shape, jnp.bfloat16),
        ],
        compiler_params=pltpu.CompilerParams(
            dimension_semantics=("arbitrary",), vmem_limit_bytes=48 * 2**20
        ),
        cost_estimate=pl.CostEstimate(
            flops=pairs * 5 * tile * tile * HD,
            bytes_accessed=4 * kv.size + 6 * q.size,
            transcendentals=pairs * tile * tile // 2,
        ),
        name="attend",
    )(vis, q, g, kv)


def neighbours():
    seq = lax.axis_index("seq")
    row, slab = lax.rem(seq, GH), lax.div(seq, GH)
    slabs = lax.axis_size("seq") // GH
    return (
        (row > 0, seq - 1),
        (row < GH - 1, seq + 1),
        (slab > 0, seq - GH),
        (slab < slabs - 1, seq + GH),
    )


def far_row():
    row = lax.rem(lax.axis_index("seq"), GH)
    odd = lax.rem(row, 2)
    exists = jnp.where(odd == 1, row < GH - 1, row > 0)
    return exists, 2 * odd


def greet(partners, peers):
    barrier = pltpu.get_barrier_semaphore()
    for peer in peers:
        pl.semaphore_signal(barrier, inc=1, device_id={"head": peer}, device_id_type=MESH)
    for exists, seq in partners:

        @pl.when(exists)
        def _():
            pl.semaphore_signal(barrier, inc=1, device_id={"seq": seq}, device_id_type=MESH)

    count = sum(exists.astype(jnp.int32) for exists, _ in partners)
    pl.semaphore_wait(barrier, count + len(peers))


def remote(src, dst, sems, index, device):
    return pltpu.make_async_remote_copy(
        src_ref=src,
        dst_ref=dst,
        send_sem=sems[0].at[index],
        recv_sem=sems[1].at[index],
        device_id=device,
        device_id_type=MESH,
    )


def for_heads(heads, body):
    def step(n, carry):
        body(n)
        return carry

    lax.fori_loop(0, heads, step, 0)


def gather_kernel(
    nh, q_in, k_in, v_in, g_in, q_out, g_out, kv_out, own, swap_s, swap_r, near_s, near_r
):
    heads, _, _, _, tile, _ = kv_out.shape
    rows = q_in.shape[0]
    h = lax.axis_index("head")
    partners = neighbours()
    up, down, before, after = partners
    peers = [lax.rem(h + j, nh) for j in range(1, nh)]
    senders = [lax.rem(h + nh - j, nh) for j in range(1, nh)]
    sources = (k_in, v_in, q_in, g_in)
    far_exists, far = far_row()
    share = nh // 2

    def place(array, n, owner):
        if array < 2:
            offset = pl.multiple_of(lax.rem(owner, share) * rows, rows)
            return kv_out.at[n, array, 1, 1 + lax.div(owner, share), pl.ds(offset, rows)]
        out = q_out if array == 2 else g_out
        return out.at[n, pl.ds(pl.multiple_of(owner * rows, rows), rows)]

    def columns(array, n, owner):
        start = pl.multiple_of((owner * heads + n) * HD, HD)
        return sources[array].at[:, pl.ds(start, HD)]

    def kept(array, n):
        return pltpu.make_async_copy(columns(array, n, h), place(array, n, h), own.at[array, n])

    def swapped(array, n, j, owner):
        return remote(
            columns(array, n, peers[j]),
            place(array, n, owner),
            (swap_s, swap_r),
            (array, j, n),
            {"head": peers[j]},
        )

    def start_swap(arrays, n):
        for array in arrays:
            for j in range(nh - 1):
                swapped(array, n, j, h).start()
            kept(array, n).start()

    def wait_swap(arrays, n):
        for array in arrays:
            for j in range(nh - 1):
                swapped(array, n, j, senders[j]).wait_recv()
            kept(array, n).wait()

    def block(n, row, first, count):
        return kv_out.at[n, :, row, pl.ds(first, count)]

    def copies(kind, n):
        if kind == 0:
            mine, plan = (1, 1, 2), ((up, (2, 1, 2), (0, 1, 2)), (down, (0, 1, 2), (2, 1, 2)))
        elif kind == 1:
            plan = ((before, (1, 3, 1), (1, 0, 1)), (after, (1, 0, 1), (1, 3, 1)))
        else:
            time = 0 if kind == 2 else 3
            plan = ((up, (2, time, 1), (0, time, 1)), (down, (0, time, 1), (2, time, 1)))
        found = []
        for side, (partner, there, here) in enumerate(plan):
            exists = partner[0]
            if kind == 2:
                exists = jnp.logical_and(exists, far != 2 * side)
            if kind == 1:
                mine = (1, 1 + side, 1)
            elif kind > 1:
                mine = (1, time, 1)
            device = {"seq": partner[1]}
            send = functools.partial(
                remote,
                block(n, *mine), block(n, *there), (near_s, near_r), (kind, side, n), device
            )
            arrive = functools.partial(
                remote,
                block(n, *mine), block(n, *here), (near_s, near_r), (kind, 1 - side, n), device
            )
            found.append((exists, send, arrive))
        return found

    def diagonal(n):
        device = {"seq": after[1]}
        return remote(
            block(n, far, 2, 1), block(n, far, 0, 1), (near_s, near_r), (4, 0, n), device
        )

    sends_diagonal = jnp.logical_and(after[0], far_exists)
    gets_diagonal = jnp.logical_and(before[0], far_exists)

    def each(kind, n, act):
        for exists, send, arrive in copies(kind, n):

            @pl.when(exists)
            def _():
                act(send, arrive)

    def start(send, arrive):
        send().start()

    greet(partners, peers)
    for_heads(heads, lambda n: start_swap((0, 1), n))

    def forward(n):
        each(0, n, lambda send, arrive: arrive().wait_recv())

        @pl.when(sends_diagonal)
        def _():
            diagonal(n).start()

        for exists_side, kind in ((0, 2), (1, 3)):
            exists, _, arrive = copies(1, n)[exists_side]

            @pl.when(exists)
            def _():
                arrive().wait_recv()
                each(kind, n, start)

    def stage(n):
        wait_swap((0, 1), n)
        each(0, n, start)
        each(1, n, start)
        start_swap((2, 3), n)

        @pl.when(n >= lag)
        def _():
            forward(n - lag)

    lag = min(2, heads)
    for_heads(heads, stage)
    for_heads(lag, lambda n: forward(heads - lag + n))

    def finish(n):
        wait_swap((2, 3), n)
        for array in range(4):
            for j in range(nh - 1):
                swapped(array, n, j, h).wait_send()
        each(0, n, lambda send, arrive: send().wait_send())
        each(1, n, lambda send, arrive: send().wait_send())

        @pl.when(sends_diagonal)
        def _():
            diagonal(n).wait_send()

        @pl.when(gets_diagonal)
        def _():
            diagonal(n).wait_recv()

        for partner, kind in ((before, 2), (after, 3)):

            @pl.when(partner[0])
            def _():
                each(kind, n, lambda send, arrive: (send().wait_send(), arrive().wait_recv()))

    for_heads(heads, finish)


def exchange_in(queries, keys, values, out_grad):
    nh = lax.axis_size("head")
    rows, width = queries.shape
    heads, tile = width // HD // nh, rows * nh // 2
    dma = pltpu.SemaphoreType.DMA
    return pl.pallas_call(
        functools.partial(gather_kernel, nh),
        in_specs=[pl.BlockSpec(memory_space=pl.ANY)] * 4,
        out_specs=[pl.BlockSpec(memory_space=pl.ANY)] * 3,
        out_shape=[
            jax.ShapeDtypeStruct((heads, 2 * tile, HD), jnp.bfloat16),
            jax.ShapeDtypeStruct((heads, 2 * tile, HD), jnp.bfloat16),
            jax.ShapeDtypeStruct((heads, 2, 3, 4, tile, HD), jnp.bfloat16),
        ],
        scratch_shapes=[
            dma((4, heads)),
            dma((4, nh - 1, heads)),
            dma((4, nh - 1, heads)),
            dma((5, 2, heads)),
            dma((5, 2, heads)),
        ],
        compiler_params=pltpu.CompilerParams(collective_id=0, has_side_effects=True),
        name="gather",
    )(queries, keys, values, out_grad)


def scatter_kernel(
    nh,
    dq_in,
    dkv_in,
    dq_out,
    dk_out,
    dv_out,
    mine,
    sides,
    edges,
    times,
    final,
    load,
    own,
    swap_s,
    swap_r,
    near_s,
    near_r,
):
    heads, _, _, _, tile, _ = dkv_in.shape
    rows = dq_out.shape[0]
    h = lax.axis_index("head")
    partners = neighbours()
    up, down, before, after = partners
    peers = [lax.rem(h + j, nh) for j in range(1, nh)]
    senders = [lax.rem(h + nh - j, nh) for j in range(1, nh)]
    outs = (dk_out, dv_out, dq_out)

    def part(array, n, owner):
        span = pl.ds(pl.multiple_of(owner * rows, rows), rows)
        return dq_in.at[n, span] if array == 2 else final.at[n, array, span]

    def columns(array, n, owner):
        start = pl.multiple_of((owner * heads + n) * HD, HD)
        return outs[array].at[:, pl.ds(start, HD)]

    def kept(array, n):
        return pltpu.make_async_copy(part(array, n, h), columns(array, n, h), own.at[array, n])

    def swapped(array, n, j, owner):
        return remote(
            part(array, n, peers[j]),
            columns(array, n, owner),
            (swap_s, swap_r),
            (array, j, n),
            {"head": peers[j]},
        )

    def start_swap(arrays, n):
        for array in arrays:
            for j in range(nh - 1):
                swapped(array, n, j, h).start()
            kept(array, n).start()

    def copies(kind, n):
        if kind == 0:
            plan = ((up, 0), (down, 1))
        else:
            plan = ((before, 0), (after, 1))
        found = []
        for partner, side in plan:
            if kind == 0:
                src, dst, here = dkv_in.at[n, :, 2 * side], sides.at[n, 1 - side], sides.at[n, side]
            else:
                src, dst, here = edges.at[n, side], times.at[n, 1 - side], times.at[n, side]
            device = {"seq": partner[1]}
            send = functools.partial(
                remote, src, dst, (near_s, near_r), (kind, side, n), device)
            arrive = functools.partial(
                remote, src, here, (near_s, near_r), (kind, 1 - side, n), device)
            found.append((partner[0], send, arrive))
        return found

    def each(kind, n, act):
        for exists, send, arrive in copies(kind, n):

            @pl.when(exists)
            def _():
                act(send, arrive)

    def loaded(n):
        return pltpu.make_async_copy(dkv_in.at[n, :, 1], mine.at[n], load.at[n])

    greet(partners, peers)

    def begin(n):
        each(0, n, lambda send, arrive: send().start())
        loaded(n).start()

    for_heads(heads, begin)
    for_heads(heads, lambda n: start_swap((2,), n))
    for buffer, pair in ((sides, (up, down)), (times, (before, after))):
        for side, partner in enumerate(pair):

            @pl.when(jnp.logical_not(partner[0]))
            def _():
                def clear(n):
                    buffer[n, side] = jnp.zeros(buffer.shape[2:], buffer.dtype)

                for_heads(heads, clear)

    def column(n, which, time):
        terms = (mine[n, which, time], sides[n, 0, which, time], sides[n, 1, which, time])
        first, second, third = (term.astype(jnp.float32) for term in terms)
        return first + second + third

    def wrap_up(n):
        each(1, n, lambda send, arrive: arrive().wait_recv())
        for which in range(2):
            for place in range(2):
                total = column(n, which, 1 + place) + times[n, place, which].astype(jnp.float32)
                final[n, which, pl.ds(place * tile, tile)] = total.astype(jnp.bfloat16)
        start_swap((0, 1), n)

    def stage(n):
        each(0, n, lambda send, arrive: arrive().wait_recv())
        loaded(n).wait()
        for which in range(2):
            for side in range(2):
                edges[n, side, which] = column(n, which, 3 * side).astype(jnp.bfloat16)
        each(1, n, lambda send, arrive: send().start())

        @pl.when(n > 0)
        def _():
            wrap_up(n - 1)

    for_heads(heads, stage)
    wrap_up(heads - 1)

    def finish(n):
        for array in range(3):
            for j in range(nh - 1):
                swapped(array, n, j, h).wait_send()
                swapped(array, n, j, senders[j]).wait_recv()
            kept(array, n).wait()
        each(0, n, lambda send, arrive: send().wait_send())
        each(1, n, lambda send, arrive: send().wait_send())

    for_heads(heads, finish)


def exchange_out(dq, dkv):
    nh = lax.axis_size("head")
    heads, rows, _ = dq.shape
    tile = rows // 2
    dma = pltpu.SemaphoreType.DMA
    whole = jax.ShapeDtypeStruct((rows // nh, nh * heads * HD), jnp.bfloat16)

    def held(*shape):
        return pltpu.VMEM(shape + (HD,), jnp.bfloat16)

    return pl.pallas_call(
        functools.partial(scatter_kernel, nh),
        in_specs=[pl.BlockSpec(memory_space=pl.ANY)] * 2,
        out_specs=[pl.BlockSpec(memory_space=pl.ANY)] * 3,
        out_shape=[whole] * 3,
        scratch_shapes=[
            held(heads, 2, 4, tile),
            held(heads, 2, 2, 4, tile),
            held(heads, 2, 2, tile),
            held(heads, 2, 2, tile),
            held(heads, 2, 2 * tile),
            dma((heads,)),
            dma((3, heads)),
            dma((3, nh - 1, heads)),
            dma((3, nh - 1, heads)),
            dma((2, 2, heads)),
            dma((2, 2, heads)),
        ],
        compiler_params=pltpu.CompilerParams(
            collective_id=1, has_side_effects=True, vmem_limit_bytes=44 * 2**20
        ),
        name="scatter",
    )(dq, dkv)


def per_device(queries, keys, values, out_grad, window):
    q, g, kv = exchange_in(queries, keys, values, out_grad)
    dq, dkv = attend(visible_slots(window, q.shape[0]), q, g, kv)
    return exchange_out(dq, dkv)


def solution(mesh):
    rows = P(("seq", "head"), None)
    return jax.shard_map(
        per_device,
        mesh=mesh,
        in_specs=(rows, rows, rows, rows, P()),
        out_specs=(rows, rows, rows),
        check_vma=False,
    )
```

```python
import functools

import jax
import jax.numpy as jnp
from jax import lax
from jax.experimental import pallas as pl
from jax.experimental.pallas import tpu as pltpu
from jax.sharding import PartitionSpec as P

HD = 128
GH = 4
SCALE = HD ** (-0.5)
LOG2E = 1.4426950408889634
MESH = pl.DeviceIdType.MESH


def visible_slots(window, heads_here):
    seq_index = lax.axis_index("seq")
    grid_time = 2 * (lax.axis_size("seq") // GH)
    reaches = lax.dynamic_slice_in_dim(window, lax.axis_index("head") * heads_here, heads_here, 0)
    slot = jnp.arange(9)
    time_off, row_off = slot // 3 - 1, slot % 3 - 1
    near_time = 2 * (seq_index // GH) + jnp.arange(2)[:, None] + time_off[None, :]
    near_row = seq_index % GH + row_off
    inside = (near_time >= 0) & (near_time < grid_time)
    inside = inside & ((near_row >= 0) & (near_row < GH))[None, :]
    reach = (jnp.abs(time_off)[None, :] <= reaches[:, :1]) & (
        jnp.abs(row_off)[None, :] <= reaches[:, 1:]
    )
    return (inside[None] & reach[:, None, :]).astype(jnp.int32).reshape(-1)


def dot(a, b, dims):
    return lax.dot_general(a, b, (dims, ((), ())), preferred_element_type=jnp.float32)


def attend_kernel(
    vis_ref, q_ref, g_ref, kv_ref, dq_ref, dkv_ref, e_scr, dp_scr, acc, dqt, tops, top, total, delta
):
    head = pl.program_id(0)
    tile = q_ref.shape[1] // 2

    def seen(qt, row, time):
        step = time - qt
        inside = jnp.logical_and(step >= 0, step < 3)
        slot = jnp.clip(step, 0, 2) * 3 + row
        return jnp.logical_and(inside, vis_ref[(head * 2 + qt) * 9 + slot] == 1)

    def one_tile(qt, carry):
        rows = pl.ds(pl.multiple_of(qt * tile, tile), tile)
        q = q_ref[0, rows, :]
        g = g_ref[0, rows, :]
        top[...] = jnp.full_like(top, -jnp.inf)
        total[...] = jnp.zeros_like(total)
        delta[...] = jnp.zeros_like(delta)
        dqt[...] = jnp.zeros_like(dqt)

        def over_visible(body):
            def step(slot, carry):
                @pl.when(vis_ref[(head * 2 + qt) * 9 + slot] == 1)
                def _():
                    body(slot, lax.rem(slot, 3), qt + lax.div(slot, 3))

                return carry

            lax.fori_loop(0, 9, step, 0)

        def scores(slot, row, time):
            s = dot(kv_ref[0, 0, row, time], q, ((1,), (1,)))
            old = top[...]
            new = jnp.maximum(old, jnp.max(s, axis=0, keepdims=True))
            shrink = jnp.exp2((old - new) * (SCALE * LOG2E))
            dp = dot(kv_ref[0, 1, row, time], g, ((1,), (1,)))
            e = jnp.exp2((s - new) * (SCALE * LOG2E))
            e_scr[slot] = e
            dp_scr[slot] = dp
            tops[slot] = new
            top[...] = new
            total[...] = total[...] * shrink + jnp.sum(e, axis=0, keepdims=True)
            delta[...] = delta[...] * shrink + jnp.sum(e * dp, axis=0, keepdims=True)

        def grads(slot, row, time):
            @pl.when(jnp.logical_or(qt == 0, jnp.logical_not(seen(0, row, time))))
            def _():
                acc[:, row, time] = jnp.zeros((2,) + acc.shape[3:], jnp.float32)

            p = e_scr[slot] * (jnp.exp2((tops[slot] - top[...]) * (SCALE * LOG2E)) * total[...])
            ds = (p * (dp_scr[slot] - delta[...])).astype(jnp.bfloat16)
            acc[1, row, time] += dot(p.astype(jnp.bfloat16), g, ((1,), (0,)))
            acc[0, row, time] += dot(ds, q, ((1,), (0,)))
            dqt[...] += dot(kv_ref[0, 0, row, time], ds, ((0,), (0,)))

        over_visible(scores)
        total[...] = 1.0 / total[...]
        delta[...] = delta[...] * total[...]
        over_visible(grads)
        dq_ref[0, rows, :] = (dqt[...] * SCALE).T.astype(jnp.bfloat16)
        return carry

    lax.fori_loop(0, 2, one_tile, 0)

    def hand_out(index, carry):
        row, time = lax.div(index, 4), lax.rem(index, 4)
        used = jnp.logical_or(seen(0, row, time), seen(1, row, time))

        @pl.when(used)
        def _():
            dkv_ref[0, 0, row, time] = (acc[0, row, time] * SCALE).astype(jnp.bfloat16)
            dkv_ref[0, 1, row, time] = acc[1, row, time].astype(jnp.bfloat16)

        @pl.when(jnp.logical_not(used))
        def _():
            dkv_ref[0, :, row, time] = jnp.zeros((2,) + acc.shape[3:], jnp.bfloat16)

        return carry

    lax.fori_loop(0, 12, hand_out, 0)


def attend(vis, q, g, kv):
    heads, rows, _ = q.shape
    tile = rows // 2
    by_head = lambda shape: pl.BlockSpec(
        (1,) + shape, lambda n, vis: (n,) + (0,) * len(shape)
    )
    pairs = heads * 18
    return pl.pallas_call(
        attend_kernel,
        grid_spec=pltpu.PrefetchScalarGridSpec(
            num_scalar_prefetch=1,
            grid=(heads,),
            in_specs=[
                by_head((rows, HD)),
                by_head((rows, HD)),
                by_head((2, 3, 4, tile, HD)),
            ],
            out_specs=[by_head((rows, HD)), by_head((2, 3, 4, tile, HD))],
            scratch_shapes=[
                pltpu.VMEM((9, tile, tile), jnp.float32),
                pltpu.VMEM((9, tile, tile), jnp.float32),
                pltpu.VMEM((2, 3, 4, tile, HD), jnp.float32),
                pltpu.VMEM((HD, tile), jnp.float32),
                pltpu.VMEM((9, 1, tile), jnp.float32),
                pltpu.VMEM((1, tile), jnp.float32),
                pltpu.VMEM((1, tile), jnp.float32),
                pltpu.VMEM((1, tile), jnp.float32),
            ],
        ),
        out_shape=[
            jax.ShapeDtypeStruct(q.shape, jnp.bfloat16),
            jax.ShapeDtypeStruct(kv.shape, jnp.bfloat16),
        ],
        compiler_params=pltpu.CompilerParams(
            dimension_semantics=("arbitrary",), vmem_limit_bytes=48 * 2**20
        ),
        cost_estimate=pl.CostEstimate(
            flops=pairs * 5 * tile * tile * HD,
            bytes_accessed=4 * kv.size + 6 * q.size,
            transcendentals=pairs * tile * tile // 2,
        ),
        name="attend",
    )(vis, q, g, kv)


def neighbours():
    seq = lax.axis_index("seq")
    row, slab = lax.rem(seq, GH), lax.div(seq, GH)
    slabs = lax.axis_size("seq") // GH
    return (
        (row > 0, seq - 1),
        (row < GH - 1, seq + 1),
        (slab > 0, seq - GH),
        (slab < slabs - 1, seq + GH),
    )


def far_row():
    row = lax.rem(lax.axis_index("seq"), GH)
    odd = lax.rem(row, 2)
    exists = jnp.where(odd == 1, row < GH - 1, row > 0)
    return exists, 2 * odd


def greet(partners, peers):
    barrier = pltpu.get_barrier_semaphore()
    for peer in peers:
        pl.semaphore_signal(barrier, inc=1, device_id={"head": peer}, device_id_type=MESH)
    for exists, seq in partners:

        @pl.when(exists)
        def _():
            pl.semaphore_signal(barrier, inc=1, device_id={"seq": seq}, device_id_type=MESH)

    count = sum(exists.astype(jnp.int32) for exists, _ in partners)
    pl.semaphore_wait(barrier, count + len(peers))


def remote(src, dst, sems, index, device):
    return pltpu.make_async_remote_copy(
        src_ref=src,
        dst_ref=dst,
        send_sem=sems[0].at[index],
        recv_sem=sems[1].at[index],
        device_id=device,
        device_id_type=MESH,
    )


def for_heads(heads, body):
    def step(n, carry):
        body(n)
        return carry

    lax.fori_loop(0, heads, step, 0)


def gather_kernel(
    nh, q_in, k_in, v_in, g_in, q_out, g_out, kv_out, own, swap_s, swap_r, near_s, near_r
):
    heads, _, _, _, tile, _ = kv_out.shape
    rows = q_in.shape[0]
    h = lax.axis_index("head")
    partners = neighbours()
    up, down, before, after = partners
    peers = [lax.rem(h + j, nh) for j in range(1, nh)]
    senders = [lax.rem(h + nh - j, nh) for j in range(1, nh)]
    sources = (k_in, v_in, q_in, g_in)
    far_exists, far = far_row()
    share = nh // 2

    def place(array, n, owner):
        if array < 2:
            offset = pl.multiple_of(lax.rem(owner, share) * rows, rows)
            return kv_out.at[n, array, 1, 1 + lax.div(owner, share), pl.ds(offset, rows)]
        out = q_out if array == 2 else g_out
        return out.at[n, pl.ds(pl.multiple_of(owner * rows, rows), rows)]

    def columns(array, n, owner):
        start = pl.multiple_of((owner * heads + n) * HD, HD)
        return sources[array].at[:, pl.ds(start, HD)]

    def kept(array, n):
        return pltpu.make_async_copy(columns(array, n, h), place(array, n, h), own.at[array, n])

    def swapped(array, n, j, owner):
        return remote(
            columns(array, n, peers[j]),
            place(array, n, owner),
            (swap_s, swap_r),
            (array, j, n),
            {"head": peers[j]},
        )

    def start_swap(arrays, n):
        for array in arrays:
            for j in range(nh - 1):
                swapped(array, n, j, h).start()
            kept(array, n).start()

    def wait_swap(arrays, n):
        for array in arrays:
            for j in range(nh - 1):
                swapped(array, n, j, senders[j]).wait_recv()
            kept(array, n).wait()

    def block(n, row, first, count):
        return kv_out.at[n, :, row, pl.ds(first, count)]

    def copies(kind, n):
        if kind == 0:
            mine, plan = (1, 1, 2), ((up, (2, 1, 2), (0, 1, 2)), (down, (0, 1, 2), (2, 1, 2)))
        elif kind == 1:
            plan = ((before, (1, 3, 1), (1, 0, 1)), (after, (1, 0, 1), (1, 3, 1)))
        else:
            time = 0 if kind == 2 else 3
            plan = ((up, (2, time, 1), (0, time, 1)), (down, (0, time, 1), (2, time, 1)))
        found = []
        for side, (partner, there, here) in enumerate(plan):
            exists = partner[0]
            if kind == 2:
                exists = jnp.logical_and(exists, far != 2 * side)
            if kind == 1:
                mine = (1, 1 + side, 1)
            elif kind > 1:
                mine = (1, time, 1)
            device = {"seq": partner[1]}
            send = functools.partial(
                remote,
                block(n, *mine), block(n, *there), (near_s, near_r), (kind, side, n), device
            )
            arrive = functools.partial(
                remote,
                block(n, *mine), block(n, *here), (near_s, near_r), (kind, 1 - side, n), device
            )
            found.append((exists, send, arrive))
        return found

    def diagonal(n):
        device = {"seq": after[1]}
        return remote(
            block(n, far, 2, 1), block(n, far, 0, 1), (near_s, near_r), (4, 0, n), device
        )

    sends_diagonal = jnp.logical_and(after[0], far_exists)
    gets_diagonal = jnp.logical_and(before[0], far_exists)

    def each(kind, n, act):
        for exists, send, arrive in copies(kind, n):

            @pl.when(exists)
            def _():
                act(send, arrive)

    def start(send, arrive):
        send().start()

    greet(partners, peers)
    ahead = min(3, heads)
    for_heads(ahead, lambda n: start_swap((0, 1), n))

    def forward(n):
        each(0, n, lambda send, arrive: arrive().wait_recv())

        @pl.when(sends_diagonal)
        def _():
            diagonal(n).start()

        for exists_side, kind in ((0, 2), (1, 3)):
            exists, _, arrive = copies(1, n)[exists_side]

            @pl.when(exists)
            def _():
                arrive().wait_recv()
                each(kind, n, start)

    def stage(n):
        wait_swap((0, 1), n)
        each(0, n, start)
        each(1, n, start)

        @pl.when(n + ahead < heads)
        def _():
            start_swap((0, 1), n + ahead)

        @pl.when(n + ahead >= heads)
        def _():
            start_swap((2, 3), n + ahead - heads)

        @pl.when(n >= lag)
        def _():
            forward(n - lag)

    lag = min(2, heads)
    for_heads(heads, stage)
    for_heads(heads - ahead, lambda n: start_swap((2, 3), ahead + n))
    for_heads(lag, lambda n: forward(heads - lag + n))

    def finish(n):
        wait_swap((2, 3), n)
        for array in range(4):
            for j in range(nh - 1):
                swapped(array, n, j, h).wait_send()
        each(0, n, lambda send, arrive: send().wait_send())
        each(1, n, lambda send, arrive: send().wait_send())

        @pl.when(sends_diagonal)
        def _():
            diagonal(n).wait_send()

        @pl.when(gets_diagonal)
        def _():
            diagonal(n).wait_recv()

        for partner, kind in ((before, 2), (after, 3)):

            @pl.when(partner[0])
            def _():
                each(kind, n, lambda send, arrive: (send().wait_send(), arrive().wait_recv()))

    for_heads(heads, finish)


def exchange_in(queries, keys, values, out_grad):
    nh = lax.axis_size("head")
    rows, width = queries.shape
    heads, tile = width // HD // nh, rows * nh // 2
    dma = pltpu.SemaphoreType.DMA
    return pl.pallas_call(
        functools.partial(gather_kernel, nh),
        in_specs=[pl.BlockSpec(memory_space=pl.ANY)] * 4,
        out_specs=[pl.BlockSpec(memory_space=pl.ANY)] * 3,
        out_shape=[
            jax.ShapeDtypeStruct((heads, 2 * tile, HD), jnp.bfloat16),
            jax.ShapeDtypeStruct((heads, 2 * tile, HD), jnp.bfloat16),
            jax.ShapeDtypeStruct((heads, 2, 3, 4, tile, HD), jnp.bfloat16),
        ],
        scratch_shapes=[
            dma((4, heads)),
            dma((4, nh - 1, heads)),
            dma((4, nh - 1, heads)),
            dma((5, 2, heads)),
            dma((5, 2, heads)),
        ],
        compiler_params=pltpu.CompilerParams(collective_id=0, has_side_effects=True),
        name="gather",
    )(queries, keys, values, out_grad)


def scatter_kernel(
    nh,
    dq_in,
    dkv_in,
    dq_out,
    dk_out,
    dv_out,
    mine,
    sides,
    edges,
    times,
    final,
    load,
    own,
    swap_s,
    swap_r,
    near_s,
    near_r,
):
    heads, _, _, _, tile, _ = dkv_in.shape
    rows = dq_out.shape[0]
    h = lax.axis_index("head")
    partners = neighbours()
    up, down, before, after = partners
    peers = [lax.rem(h + j, nh) for j in range(1, nh)]
    senders = [lax.rem(h + nh - j, nh) for j in range(1, nh)]
    outs = (dk_out, dv_out, dq_out)

    def part(array, n, owner):
        span = pl.ds(pl.multiple_of(owner * rows, rows), rows)
        return dq_in.at[n, span] if array == 2 else final.at[n, array, span]

    def columns(array, n, owner):
        start = pl.multiple_of((owner * heads + n) * HD, HD)
        return outs[array].at[:, pl.ds(start, HD)]

    def kept(array, n):
        return pltpu.make_async_copy(part(array, n, h), columns(array, n, h), own.at[array, n])

    def swapped(array, n, j, owner):
        return remote(
            part(array, n, peers[j]),
            columns(array, n, owner),
            (swap_s, swap_r),
            (array, j, n),
            {"head": peers[j]},
        )

    def start_swap(arrays, n):
        for array in arrays:
            for j in range(nh - 1):
                swapped(array, n, j, h).start()
            kept(array, n).start()

    def copies(kind, n):
        if kind == 0:
            plan = ((up, 0), (down, 1))
        else:
            plan = ((before, 0), (after, 1))
        found = []
        for partner, side in plan:
            if kind == 0:
                src, dst, here = dkv_in.at[n, :, 2 * side], sides.at[n, 1 - side], sides.at[n, side]
            else:
                src, dst, here = edges.at[n, side], times.at[n, 1 - side], times.at[n, side]
            device = {"seq": partner[1]}
            send = functools.partial(
                remote, src, dst, (near_s, near_r), (kind, side, n), device)
            arrive = functools.partial(
                remote, src, here, (near_s, near_r), (kind, 1 - side, n), device)
            found.append((partner[0], send, arrive))
        return found

    def each(kind, n, act):
        for exists, send, arrive in copies(kind, n):

            @pl.when(exists)
            def _():
                act(send, arrive)

    def loaded(n):
        return pltpu.make_async_copy(dkv_in.at[n, :, 1], mine.at[n], load.at[n])

    greet(partners, peers)

    def begin(n):
        each(0, n, lambda send, arrive: send().start())
        loaded(n).start()

    ahead = min(3, heads)
    for_heads(ahead, begin)
    for_heads(heads, lambda n: start_swap((2,), n))
    for buffer, pair in ((sides, (up, down)), (times, (before, after))):
        for side, partner in enumerate(pair):

            @pl.when(jnp.logical_not(partner[0]))
            def _():
                def clear(n):
                    buffer[n, side] = jnp.zeros(buffer.shape[2:], buffer.dtype)

                for_heads(heads, clear)

    def column(n, which, time):
        terms = (mine[n, which, time], sides[n, 0, which, time], sides[n, 1, which, time])
        first, second, third = (term.astype(jnp.float32) for term in terms)
        return first + second + third

    def wrap_up(n):
        each(1, n, lambda send, arrive: arrive().wait_recv())
        for which in range(2):
            for place in range(2):
                total = column(n, which, 1 + place) + times[n, place, which].astype(jnp.float32)
                final[n, which, pl.ds(place * tile, tile)] = total.astype(jnp.bfloat16)
        start_swap((0, 1), n)

    def stage(n):
        each(0, n, lambda send, arrive: arrive().wait_recv())
        loaded(n).wait()
        for which in range(2):
            for side in range(2):
                edges[n, side, which] = column(n, which, 3 * side).astype(jnp.bfloat16)
        each(1, n, lambda send, arrive: send().start())

        @pl.when(n + ahead < heads)
        def _():
            begin(n + ahead)

        @pl.when(n > 0)
        def _():
            wrap_up(n - 1)

    for_heads(heads, stage)
    wrap_up(heads - 1)

    def finish(n):
        for array in range(3):
            for j in range(nh - 1):
                swapped(array, n, j, h).wait_send()
                swapped(array, n, j, senders[j]).wait_recv()
            kept(array, n).wait()
        each(0, n, lambda send, arrive: send().wait_send())
        each(1, n, lambda send, arrive: send().wait_send())

    for_heads(heads, finish)


def exchange_out(dq, dkv):
    nh = lax.axis_size("head")
    heads, rows, _ = dq.shape
    tile = rows // 2
    dma = pltpu.SemaphoreType.DMA
    whole = jax.ShapeDtypeStruct((rows // nh, nh * heads * HD), jnp.bfloat16)

    def held(*shape):
        return pltpu.VMEM(shape + (HD,), jnp.bfloat16)

    return pl.pallas_call(
        functools.partial(scatter_kernel, nh),
        in_specs=[pl.BlockSpec(memory_space=pl.ANY)] * 2,
        out_specs=[pl.BlockSpec(memory_space=pl.ANY)] * 3,
        out_shape=[whole] * 3,
        scratch_shapes=[
            held(heads, 2, 4, tile),
            held(heads, 2, 2, 4, tile),
            held(heads, 2, 2, tile),
            held(heads, 2, 2, tile),
            held(heads, 2, 2 * tile),
            dma((heads,)),
            dma((3, heads)),
            dma((3, nh - 1, heads)),
            dma((3, nh - 1, heads)),
            dma((2, 2, heads)),
            dma((2, 2, heads)),
        ],
        compiler_params=pltpu.CompilerParams(
            collective_id=1, has_side_effects=True, vmem_limit_bytes=44 * 2**20
        ),
        name="scatter",
    )(dq, dkv)


def per_device(queries, keys, values, out_grad, window):
    q, g, kv = exchange_in(queries, keys, values, out_grad)
    dq, dkv = attend(visible_slots(window, q.shape[0]), q, g, kv)
    return exchange_out(dq, dkv)


def solution(mesh):
    rows = P(("seq", "head"), None)
    return jax.shard_map(
        per_device,
        mesh=mesh,
        in_specs=(rows, rows, rows, rows, P()),
        out_specs=(rows, rows, rows),
        check_vma=False,
    )
```

```python
import functools

import jax
import jax.numpy as jnp
from jax import lax
from jax.experimental import pallas as pl
from jax.experimental.pallas import tpu as pltpu
from jax.sharding import PartitionSpec as P

HD = 128
GH = 4
SCALE = HD ** (-0.5)
LOG2E = 1.4426950408889634
MESH = pl.DeviceIdType.MESH


def visible_slots(window, heads_here):
    seq_index = lax.axis_index("seq")
    grid_time = 2 * (lax.axis_size("seq") // GH)
    reaches = lax.dynamic_slice_in_dim(window, lax.axis_index("head") * heads_here, heads_here, 0)
    slot = jnp.arange(9)
    time_off, row_off = slot // 3 - 1, slot % 3 - 1
    near_time = 2 * (seq_index // GH) + jnp.arange(2)[:, None] + time_off[None, :]
    near_row = seq_index % GH + row_off
    inside = (near_time >= 0) & (near_time < grid_time)
    inside = inside & ((near_row >= 0) & (near_row < GH))[None, :]
    reach = (jnp.abs(time_off)[None, :] <= reaches[:, :1]) & (
        jnp.abs(row_off)[None, :] <= reaches[:, 1:]
    )
    return (inside[None] & reach[:, None, :]).astype(jnp.int32).reshape(-1)


def dot(a, b, dims):
    return lax.dot_general(a, b, (dims, ((), ())), preferred_element_type=jnp.float32)


def attend_kernel(
    vis_ref, q_ref, g_ref, kv_ref, dq_ref, dkv_ref, e_scr, dp_scr, acc, dqt, tops, top, total, delta
):
    head = pl.program_id(0)
    tile = q_ref.shape[1] // 2

    def seen(qt, row, time):
        step = time - qt
        inside = jnp.logical_and(step >= 0, step < 3)
        slot = jnp.clip(step, 0, 2) * 3 + row
        return jnp.logical_and(inside, vis_ref[(head * 2 + qt) * 9 + slot] == 1)

    def one_tile(qt, carry):
        rows = pl.ds(pl.multiple_of(qt * tile, tile), tile)
        q = q_ref[0, rows, :]
        g = g_ref[0, rows, :]
        top[...] = jnp.full_like(top, -jnp.inf)
        total[...] = jnp.zeros_like(total)
        delta[...] = jnp.zeros_like(delta)
        dqt[...] = jnp.zeros_like(dqt)

        def over_visible(body):
            def step(slot, carry):
                @pl.when(vis_ref[(head * 2 + qt) * 9 + slot] == 1)
                def _():
                    body(slot, lax.rem(slot, 3), qt + lax.div(slot, 3))

                return carry

            lax.fori_loop(0, 9, step, 0)

        def scores(slot, row, time):
            s = dot(kv_ref[0, 0, row, time], q, ((1,), (1,)))
            old = top[...]
            new = jnp.maximum(old, jnp.max(s, axis=0, keepdims=True))
            shrink = jnp.exp2((old - new) * (SCALE * LOG2E))
            dp = dot(kv_ref[0, 1, row, time], g, ((1,), (1,)))
            e = jnp.exp2((s - new) * (SCALE * LOG2E))
            e_scr[slot] = e
            dp_scr[slot] = dp
            tops[slot] = new
            top[...] = new
            total[...] = total[...] * shrink + jnp.sum(e, axis=0, keepdims=True)
            delta[...] = delta[...] * shrink + jnp.sum(e * dp, axis=0, keepdims=True)

        def grads(slot, row, time):
            @pl.when(jnp.logical_or(qt == 0, jnp.logical_not(seen(0, row, time))))
            def _():
                acc[:, row, time] = jnp.zeros((2,) + acc.shape[3:], jnp.float32)

            p = e_scr[slot] * (jnp.exp2((tops[slot] - top[...]) * (SCALE * LOG2E)) * total[...])
            ds = (p * (dp_scr[slot] - delta[...])).astype(jnp.bfloat16)
            acc[1, row, time] += dot(p.astype(jnp.bfloat16), g, ((1,), (0,)))
            acc[0, row, time] += dot(ds, q, ((1,), (0,)))
            dqt[...] += dot(kv_ref[0, 0, row, time], ds, ((0,), (0,)))

        over_visible(scores)
        total[...] = 1.0 / total[...]
        delta[...] = delta[...] * total[...]
        over_visible(grads)
        dq_ref[0, rows, :] = (dqt[...] * SCALE).T.astype(jnp.bfloat16)
        return carry

    lax.fori_loop(0, 2, one_tile, 0)

    def hand_out(index, carry):
        row, time = lax.div(index, 4), lax.rem(index, 4)
        used = jnp.logical_or(seen(0, row, time), seen(1, row, time))

        @pl.when(used)
        def _():
            dkv_ref[0, 0, row, time] = (acc[0, row, time] * SCALE).astype(jnp.bfloat16)
            dkv_ref[0, 1, row, time] = acc[1, row, time].astype(jnp.bfloat16)

        @pl.when(jnp.logical_not(used))
        def _():
            dkv_ref[0, :, row, time] = jnp.zeros((2,) + acc.shape[3:], jnp.bfloat16)

        return carry

    lax.fori_loop(0, 12, hand_out, 0)


def attend(vis, q, g, kv):
    heads, rows, _ = q.shape
    tile = rows // 2
    by_head = lambda shape: pl.BlockSpec(
        (1,) + shape, lambda n, vis: (n,) + (0,) * len(shape)
    )
    pairs = heads * 18
    return pl.pallas_call(
        attend_kernel,
        grid_spec=pltpu.PrefetchScalarGridSpec(
            num_scalar_prefetch=1,
            grid=(heads,),
            in_specs=[
                by_head((rows, HD)),
                by_head((rows, HD)),
                by_head((2, 3, 4, tile, HD)),
            ],
            out_specs=[by_head((rows, HD)), by_head((2, 3, 4, tile, HD))],
            scratch_shapes=[
                pltpu.VMEM((9, tile, tile), jnp.float32),
                pltpu.VMEM((9, tile, tile), jnp.float32),
                pltpu.VMEM((2, 3, 4, tile, HD), jnp.float32),
                pltpu.VMEM((HD, tile), jnp.float32),
                pltpu.VMEM((9, 1, tile), jnp.float32),
                pltpu.VMEM((1, tile), jnp.float32),
                pltpu.VMEM((1, tile), jnp.float32),
                pltpu.VMEM((1, tile), jnp.float32),
            ],
        ),
        out_shape=[
            jax.ShapeDtypeStruct(q.shape, jnp.bfloat16),
            jax.ShapeDtypeStruct(kv.shape, jnp.bfloat16),
        ],
        compiler_params=pltpu.CompilerParams(
            dimension_semantics=("arbitrary",), vmem_limit_bytes=48 * 2**20
        ),
        cost_estimate=pl.CostEstimate(
            flops=pairs * 5 * tile * tile * HD,
            bytes_accessed=4 * kv.size + 6 * q.size,
            transcendentals=pairs * tile * tile // 2,
        ),
        name="attend",
    )(vis, q, g, kv)


def neighbours():
    seq = lax.axis_index("seq")
    row, slab = lax.rem(seq, GH), lax.div(seq, GH)
    slabs = lax.axis_size("seq") // GH
    return (
        (row > 0, seq - 1),
        (row < GH - 1, seq + 1),
        (slab > 0, seq - GH),
        (slab < slabs - 1, seq + GH),
    )


def far_row():
    row = lax.rem(lax.axis_index("seq"), GH)
    odd = lax.rem(row, 2)
    exists = jnp.where(odd == 1, row < GH - 1, row > 0)
    return exists, 2 * odd


def greet(partners, peers):
    barrier = pltpu.get_barrier_semaphore()
    for peer in peers:
        pl.semaphore_signal(barrier, inc=1, device_id={"head": peer}, device_id_type=MESH)
    for exists, seq in partners:

        @pl.when(exists)
        def _():
            pl.semaphore_signal(barrier, inc=1, device_id={"seq": seq}, device_id_type=MESH)

    count = sum(exists.astype(jnp.int32) for exists, _ in partners)
    pl.semaphore_wait(barrier, count + len(peers))


def remote(src, dst, sems, index, device):
    return pltpu.make_async_remote_copy(
        src_ref=src,
        dst_ref=dst,
        send_sem=sems[0].at[index],
        recv_sem=sems[1].at[index],
        device_id=device,
        device_id_type=MESH,
    )


def for_heads(heads, body):
    def step(n, carry):
        body(n)
        return carry

    lax.fori_loop(0, heads, step, 0)


def gather_kernel(
    nh, q_in, k_in, v_in, g_in, q_out, g_out, kv_out, stage_buf, load, own, swap_s, swap_r, near_s, near_r
):
    heads, _, _, _, tile, _ = kv_out.shape
    rows = q_in.shape[0]
    h = lax.axis_index("head")
    partners = neighbours()
    up, down, before, after = partners
    peers = [lax.rem(h + j, nh) for j in range(1, nh)]
    senders = [lax.rem(h + nh - j, nh) for j in range(1, nh)]
    sources = (k_in, v_in, q_in, g_in)
    far_exists, far = far_row()
    share = nh // 2

    def place(array, n, owner):
        if array < 2:
            offset = pl.multiple_of(lax.rem(owner, share) * rows, rows)
            return kv_out.at[n, array, 1, 1 + lax.div(owner, share), pl.ds(offset, rows)]
        out = q_out if array == 2 else g_out
        return out.at[n, pl.ds(pl.multiple_of(owner * rows, rows), rows)]

    def columns(array, n, owner):
        start = pl.multiple_of((owner * heads + n) * HD, HD)
        return sources[array].at[:, pl.ds(start, HD)]

    def staged(array, n, owner):
        return stage_buf.at[array, owner * heads + n]

    def loaded(array, n, owner):
        return pltpu.make_async_copy(
            columns(array, n, owner), staged(array, n, owner), load.at[array, owner * heads + n]
        )

    def kept(array, n):
        return pltpu.make_async_copy(staged(array, n, h), place(array, n, h), own.at[array, n])

    def swapped(array, n, j, owner):
        return remote(
            staged(array, n, peers[j]),
            place(array, n, owner),
            (swap_s, swap_r),
            (array, j, n),
            {"head": peers[j]},
        )

    def start_load(arrays, n):
        for array in arrays:
            for owner in peers + [h]:
                loaded(array, n, owner).start()

    def start_swap(arrays, n):
        for array in arrays:
            for j in range(nh - 1):
                loaded(array, n, peers[j]).wait()
                swapped(array, n, j, h).start()
            loaded(array, n, h).wait()
            kept(array, n).start()

    def wait_swap(arrays, n):
        for array in arrays:
            for j in range(nh - 1):
                swapped(array, n, j, senders[j]).wait_recv()
            kept(array, n).wait()

    def block(n, row, first, count):
        return kv_out.at[n, :, row, pl.ds(first, count)]

    def copies(kind, n):
        if kind == 0:
            mine, plan = (1, 1, 2), ((up, (2, 1, 2), (0, 1, 2)), (down, (0, 1, 2), (2, 1, 2)))
        elif kind == 1:
            plan = ((before, (1, 3, 1), (1, 0, 1)), (after, (1, 0, 1), (1, 3, 1)))
        else:
            time = 0 if kind == 2 else 3
            plan = ((up, (2, time, 1), (0, time, 1)), (down, (0, time, 1), (2, time, 1)))
        found = []
        for side, (partner, there, here) in enumerate(plan):
            exists = partner[0]
            if kind == 2:
                exists = jnp.logical_and(exists, far != 2 * side)
            if kind == 1:
                mine = (1, 1 + side, 1)
            elif kind > 1:
                mine = (1, time, 1)
            device = {"seq": partner[1]}
            send = functools.partial(
                remote,
                block(n, *mine), block(n, *there), (near_s, near_r), (kind, side, n), device
            )
            arrive = functools.partial(
                remote,
                block(n, *mine), block(n, *here), (near_s, near_r), (kind, 1 - side, n), device
            )
            found.append((exists, send, arrive))
        return found

    def diagonal(n):
        device = {"seq": after[1]}
        return remote(
            block(n, far, 2, 1), block(n, far, 0, 1), (near_s, near_r), (4, 0, n), device
        )

    sends_diagonal = jnp.logical_and(after[0], far_exists)
    gets_diagonal = jnp.logical_and(before[0], far_exists)

    def each(kind, n, act):
        for exists, send, arrive in copies(kind, n):

            @pl.when(exists)
            def _():
                act(send, arrive)

    def start(send, arrive):
        send().start()

    for_heads(heads, lambda n: start_load((0, 1), n))
    for_heads(heads, lambda n: start_load((2, 3), n))
    greet(partners, peers)
    ahead = min(3, heads)
    for_heads(ahead, lambda n: start_swap((0, 1), n))

    def forward(n):
        each(0, n, lambda send, arrive: arrive().wait_recv())

        @pl.when(sends_diagonal)
        def _():
            diagonal(n).start()

        for exists_side, kind in ((0, 2), (1, 3)):
            exists, _, arrive = copies(1, n)[exists_side]

            @pl.when(exists)
            def _():
                arrive().wait_recv()
                each(kind, n, start)

    def stage(n):
        wait_swap((0, 1), n)
        each(0, n, start)
        each(1, n, start)

        @pl.when(n + ahead < heads)
        def _():
            start_swap((0, 1), n + ahead)

        @pl.when(n + ahead >= heads)
        def _():
            start_swap((2, 3), n + ahead - heads)

        @pl.when(n >= lag)
        def _():
            forward(n - lag)

    lag = min(2, heads)
    for_heads(heads, stage)
    for_heads(heads - ahead, lambda n: start_swap((2, 3), ahead + n))
    for_heads(lag, lambda n: forward(heads - lag + n))

    def finish(n):
        wait_swap((2, 3), n)
        for array in range(4):
            for j in range(nh - 1):
                swapped(array, n, j, h).wait_send()
        each(0, n, lambda send, arrive: send().wait_send())
        each(1, n, lambda send, arrive: send().wait_send())

        @pl.when(sends_diagonal)
        def _():
            diagonal(n).wait_send()

        @pl.when(gets_diagonal)
        def _():
            diagonal(n).wait_recv()

        for partner, kind in ((before, 2), (after, 3)):

            @pl.when(partner[0])
            def _():
                each(kind, n, lambda send, arrive: (send().wait_send(), arrive().wait_recv()))

    for_heads(heads, finish)


def exchange_in(queries, keys, values, out_grad):
    nh = lax.axis_size("head")
    rows, width = queries.shape
    heads, tile = width // HD // nh, rows * nh // 2
    dma = pltpu.SemaphoreType.DMA
    return pl.pallas_call(
        functools.partial(gather_kernel, nh),
        in_specs=[pl.BlockSpec(memory_space=pl.ANY)] * 4,
        out_specs=[pl.BlockSpec(memory_space=pl.ANY)] * 3,
        out_shape=[
            jax.ShapeDtypeStruct((heads, 2 * tile, HD), jnp.bfloat16),
            jax.ShapeDtypeStruct((heads, 2 * tile, HD), jnp.bfloat16),
            jax.ShapeDtypeStruct((heads, 2, 3, 4, tile, HD), jnp.bfloat16),
        ],
        scratch_shapes=[
            pltpu.VMEM((4, nh * heads, rows, HD), jnp.bfloat16),
            dma((4, nh * heads)),
            dma((4, heads)),
            dma((4, nh - 1, heads)),
            dma((4, nh - 1, heads)),
            dma((5, 2, heads)),
            dma((5, 2, heads)),
        ],
        compiler_params=pltpu.CompilerParams(
            collective_id=0, has_side_effects=True, vmem_limit_bytes=44 * 2**20
        ),
        name="gather",
    )(queries, keys, values, out_grad)


def scatter_kernel(
    nh,
    dq_in,
    dkv_in,
    dq_out,
    dk_out,
    dv_out,
    mine,
    sides,
    edges,
    times,
    final,
    landed,
    load,
    pull,
    push,
    swap_s,
    swap_r,
    near_s,
    near_r,
):
    heads, _, _, _, tile, _ = dkv_in.shape
    rows = dq_out.shape[0]
    h = lax.axis_index("head")
    partners = neighbours()
    up, down, before, after = partners
    peers = [lax.rem(h + j, nh) for j in range(1, nh)]
    senders = [lax.rem(h + nh - j, nh) for j in range(1, nh)]
    outs = (dk_out, dv_out, dq_out)

    def part(array, n, owner):
        span = pl.ds(pl.multiple_of(owner * rows, rows), rows)
        return dq_in.at[n, span] if array == 2 else final.at[n, array, span]

    def columns(array, n, owner):
        start = pl.multiple_of((owner * heads + n) * HD, HD)
        return outs[array].at[:, pl.ds(start, HD)]

    def pulled(n):
        return pltpu.make_async_copy(part(2, n, h), landed.at[2, h * heads + n], pull.at[n])

    def stored(array, n, owner):
        place = owner * heads + n
        src = landed.at[array, place]
        if array < 2 and owner is h:
            src = part(array, n, h)
        return pltpu.make_async_copy(src, columns(array, n, owner), push.at[array, place])

    def swapped(array, n, j, owner):
        return remote(
            part(array, n, peers[j]),
            landed.at[array, owner * heads + n],
            (swap_s, swap_r),
            (array, j, n),
            {"head": peers[j]},
        )

    def start_swap(arrays, n):
        for array in arrays:
            for j in range(nh - 1):
                swapped(array, n, j, h).start()
            if array == 2:
                pulled(n).start()
            else:
                stored(array, n, h).start()

    def settle(arrays, n):
        for array in arrays:
            if array == 2:
                pulled(n).wait()
                stored(array, n, h).start()
            for j in range(nh - 1):
                swapped(array, n, j, senders[j]).wait_recv()
                stored(array, n, senders[j]).start()

    def copies(kind, n):
        if kind == 0:
            plan = ((up, 0), (down, 1))
        else:
            plan = ((before, 0), (after, 1))
        found = []
        for partner, side in plan:
            if kind == 0:
                src, dst, here = dkv_in.at[n, :, 2 * side], sides.at[n, 1 - side], sides.at[n, side]
            else:
                src, dst, here = edges.at[n, side], times.at[n, 1 - side], times.at[n, side]
            device = {"seq": partner[1]}
            send = functools.partial(
                remote, src, dst, (near_s, near_r), (kind, side, n), device)
            arrive = functools.partial(
                remote, src, here, (near_s, near_r), (kind, 1 - side, n), device)
            found.append((partner[0], send, arrive))
        return found

    def each(kind, n, act):
        for exists, send, arrive in copies(kind, n):

            @pl.when(exists)
            def _():
                act(send, arrive)

    def loaded(n):
        return pltpu.make_async_copy(dkv_in.at[n, :, 1], mine.at[n], load.at[n])

    greet(partners, peers)

    def begin(n):
        each(0, n, lambda send, arrive: send().start())
        loaded(n).start()

    ahead = min(3, heads)
    for_heads(ahead, begin)
    for_heads(heads, lambda n: start_swap((2,), n))
    for buffer, pair in ((sides, (up, down)), (times, (before, after))):
        for side, partner in enumerate(pair):

            @pl.when(jnp.logical_not(partner[0]))
            def _():
                def clear(n):
                    buffer[n, side] = jnp.zeros(buffer.shape[2:], buffer.dtype)

                for_heads(heads, clear)

    def column(n, which, time):
        terms = (mine[n, which, time], sides[n, 0, which, time], sides[n, 1, which, time])
        first, second, third = (term.astype(jnp.float32) for term in terms)
        return first + second + third

    def wrap_up(n):
        each(1, n, lambda send, arrive: arrive().wait_recv())
        for which in range(2):
            for place in range(2):
                total = column(n, which, 1 + place) + times[n, place, which].astype(jnp.float32)
                final[n, which, pl.ds(place * tile, tile)] = total.astype(jnp.bfloat16)
        start_swap((0, 1), n)
        settle((2,), n)

        @pl.when(n >= lag)
        def _():
            settle((0, 1), n - lag)

    lag = min(2, heads)

    def stage(n):
        each(0, n, lambda send, arrive: arrive().wait_recv())
        loaded(n).wait()
        for which in range(2):
            for side in range(2):
                edges[n, side, which] = column(n, which, 3 * side).astype(jnp.bfloat16)
        each(1, n, lambda send, arrive: send().start())

        @pl.when(n + ahead < heads)
        def _():
            begin(n + ahead)

        @pl.when(n > 0)
        def _():
            wrap_up(n - 1)

    for_heads(heads, stage)
    wrap_up(heads - 1)
    for_heads(lag, lambda n: settle((0, 1), heads - lag + n))

    def finish(n):
        for array in range(3):
            for j in range(nh - 1):
                swapped(array, n, j, h).wait_send()
                stored(array, n, senders[j]).wait()
            stored(array, n, h).wait()
        each(0, n, lambda send, arrive: send().wait_send())
        each(1, n, lambda send, arrive: send().wait_send())

    for_heads(heads, finish)


def exchange_out(dq, dkv):
    nh = lax.axis_size("head")
    heads, rows, _ = dq.shape
    tile = rows // 2
    dma = pltpu.SemaphoreType.DMA
    whole = jax.ShapeDtypeStruct((rows // nh, nh * heads * HD), jnp.bfloat16)

    def held(*shape):
        return pltpu.VMEM(shape + (HD,), jnp.bfloat16)

    return pl.pallas_call(
        functools.partial(scatter_kernel, nh),
        in_specs=[pl.BlockSpec(memory_space=pl.ANY)] * 2,
        out_specs=[pl.BlockSpec(memory_space=pl.ANY)] * 3,
        out_shape=[whole] * 3,
        scratch_shapes=[
            held(heads, 2, 4, tile),
            held(heads, 2, 2, 4, tile),
            held(heads, 2, 2, tile),
            held(heads, 2, 2, tile),
            held(heads, 2, 2 * tile),
            held(3, nh * heads, rows // nh),
            dma((heads,)),
            dma((heads,)),
            dma((3, nh * heads)),
            dma((3, nh - 1, heads)),
            dma((3, nh - 1, heads)),
            dma((2, 2, heads)),
            dma((2, 2, heads)),
        ],
        compiler_params=pltpu.CompilerParams(
            collective_id=1, has_side_effects=True, vmem_limit_bytes=44 * 2**20
        ),
        name="scatter",
    )(dq, dkv)


def per_device(queries, keys, values, out_grad, window):
    q, g, kv = exchange_in(queries, keys, values, out_grad)
    dq, dkv = attend(visible_slots(window, q.shape[0]), q, g, kv)
    return exchange_out(dq, dkv)


def solution(mesh):
    rows = P(("seq", "head"), None)
    return jax.shard_map(
        per_device,
        mesh=mesh,
        in_specs=(rows, rows, rows, rows, P()),
        out_specs=(rows, rows, rows),
        check_vma=False,
    )
```

```python
import functools

import jax
import jax.numpy as jnp
from jax import lax
from jax.experimental import pallas as pl
from jax.experimental.pallas import tpu as pltpu
from jax.sharding import PartitionSpec as P

HD = 128
GH = 4
SCALE = HD ** (-0.5)
LOG2E = 1.4426950408889634
MESH = pl.DeviceIdType.MESH


def visible_slots(window, heads_here):
    seq_index = lax.axis_index("seq")
    grid_time = 2 * (lax.axis_size("seq") // GH)
    reaches = lax.dynamic_slice_in_dim(window, lax.axis_index("head") * heads_here, heads_here, 0)
    slot = jnp.arange(9)
    time_off, row_off = slot // 3 - 1, slot % 3 - 1
    near_time = 2 * (seq_index // GH) + jnp.arange(2)[:, None] + time_off[None, :]
    near_row = seq_index % GH + row_off
    inside = (near_time >= 0) & (near_time < grid_time)
    inside = inside & ((near_row >= 0) & (near_row < GH))[None, :]
    reach = (jnp.abs(time_off)[None, :] <= reaches[:, :1]) & (
        jnp.abs(row_off)[None, :] <= reaches[:, 1:]
    )
    return (inside[None] & reach[:, None, :]).astype(jnp.int32).reshape(-1)


def dot(a, b, dims):
    return lax.dot_general(a, b, (dims, ((), ())), preferred_element_type=jnp.float32)


def attend_kernel(
    vis_ref, q_ref, g_ref, kv_ref, dq_ref, dkv_ref, e_scr, dp_scr, acc, dqt, tops, top, total, delta
):
    head = pl.program_id(0)
    tile = q_ref.shape[1] // 2

    def seen(qt, row, time):
        step = time - qt
        inside = jnp.logical_and(step >= 0, step < 3)
        slot = jnp.clip(step, 0, 2) * 3 + row
        return jnp.logical_and(inside, vis_ref[(head * 2 + qt) * 9 + slot] == 1)

    def one_tile(qt, carry):
        rows = pl.ds(pl.multiple_of(qt * tile, tile), tile)
        q = q_ref[0, rows, :]
        g = g_ref[0, rows, :]
        top[...] = jnp.full_like(top, -jnp.inf)
        total[...] = jnp.zeros_like(total)
        delta[...] = jnp.zeros_like(delta)
        dqt[...] = jnp.zeros_like(dqt)

        def over_visible(body):
            def step(slot, carry):
                @pl.when(vis_ref[(head * 2 + qt) * 9 + slot] == 1)
                def _():
                    body(slot, lax.rem(slot, 3), qt + lax.div(slot, 3))

                return carry

            lax.fori_loop(0, 9, step, 0)

        def scores(slot, row, time):
            s = dot(kv_ref[0, 0, row, time], q, ((1,), (1,)))
            old = top[...]
            new = jnp.maximum(old, jnp.max(s, axis=0, keepdims=True))
            shrink = jnp.exp2((old - new) * (SCALE * LOG2E))
            dp = dot(kv_ref[0, 1, row, time], g, ((1,), (1,)))
            e = jnp.exp2((s - new) * (SCALE * LOG2E))
            e_scr[slot] = e
            dp_scr[slot] = dp
            tops[slot] = new
            top[...] = new
            total[...] = total[...] * shrink + jnp.sum(e, axis=0, keepdims=True)
            delta[...] = delta[...] * shrink + jnp.sum(e * dp, axis=0, keepdims=True)

        def grads(slot, row, time):
            @pl.when(jnp.logical_or(qt == 0, jnp.logical_not(seen(0, row, time))))
            def _():
                acc[:, row, time] = jnp.zeros((2,) + acc.shape[3:], jnp.float32)

            p = e_scr[slot] * (jnp.exp2((tops[slot] - top[...]) * (SCALE * LOG2E)) * total[...])
            ds = (p * (dp_scr[slot] - delta[...])).astype(jnp.bfloat16)
            acc[1, row, time] += dot(p.astype(jnp.bfloat16), g, ((1,), (0,)))
            acc[0, row, time] += dot(ds, q, ((1,), (0,)))
            dqt[...] += dot(kv_ref[0, 0, row, time], ds, ((0,), (0,)))

        over_visible(scores)
        total[...] = 1.0 / total[...]
        delta[...] = delta[...] * total[...]
        over_visible(grads)
        dq_ref[0, rows, :] = (dqt[...] * SCALE).T.astype(jnp.bfloat16)
        return carry

    lax.fori_loop(0, 2, one_tile, 0)

    def hand_out(index, carry):
        row, time = lax.div(index, 4), lax.rem(index, 4)
        used = jnp.logical_or(seen(0, row, time), seen(1, row, time))

        @pl.when(used)
        def _():
            dkv_ref[0, 0, row, time] = (acc[0, row, time] * SCALE).astype(jnp.bfloat16)
            dkv_ref[0, 1, row, time] = acc[1, row, time].astype(jnp.bfloat16)

        @pl.when(jnp.logical_not(used))
        def _():
            dkv_ref[0, :, row, time] = jnp.zeros((2,) + acc.shape[3:], jnp.bfloat16)

        return carry

    lax.fori_loop(0, 12, hand_out, 0)


def attend(vis, q, g, kv):
    heads, rows, _ = q.shape
    tile = rows // 2
    by_head = lambda shape: pl.BlockSpec(
        (1,) + shape, lambda n, vis: (n,) + (0,) * len(shape)
    )
    pairs = heads * 18
    return pl.pallas_call(
        attend_kernel,
        grid_spec=pltpu.PrefetchScalarGridSpec(
            num_scalar_prefetch=1,
            grid=(heads,),
            in_specs=[
                by_head((rows, HD)),
                by_head((rows, HD)),
                by_head((2, 3, 4, tile, HD)),
            ],
            out_specs=[by_head((rows, HD)), by_head((2, 3, 4, tile, HD))],
            scratch_shapes=[
                pltpu.VMEM((9, tile, tile), jnp.float32),
                pltpu.VMEM((9, tile, tile), jnp.float32),
                pltpu.VMEM((2, 3, 4, tile, HD), jnp.float32),
                pltpu.VMEM((HD, tile), jnp.float32),
                pltpu.VMEM((9, 1, tile), jnp.float32),
                pltpu.VMEM((1, tile), jnp.float32),
                pltpu.VMEM((1, tile), jnp.float32),
                pltpu.VMEM((1, tile), jnp.float32),
            ],
        ),
        out_shape=[
            jax.ShapeDtypeStruct(q.shape, jnp.bfloat16),
            jax.ShapeDtypeStruct(kv.shape, jnp.bfloat16),
        ],
        compiler_params=pltpu.CompilerParams(
            dimension_semantics=("arbitrary",), vmem_limit_bytes=48 * 2**20
        ),
        cost_estimate=pl.CostEstimate(
            flops=pairs * 5 * tile * tile * HD,
            bytes_accessed=4 * kv.size + 6 * q.size,
            transcendentals=pairs * tile * tile // 2,
        ),
        name="attend",
    )(vis, q, g, kv)


def neighbours():
    seq = lax.axis_index("seq")
    row, slab = lax.rem(seq, GH), lax.div(seq, GH)
    slabs = lax.axis_size("seq") // GH
    return (
        (row > 0, seq - 1),
        (row < GH - 1, seq + 1),
        (slab > 0, seq - GH),
        (slab < slabs - 1, seq + GH),
    )


def far_row():
    row = lax.rem(lax.axis_index("seq"), GH)
    odd = lax.rem(row, 2)
    exists = jnp.where(odd == 1, row < GH - 1, row > 0)
    return exists, 2 * odd


def greet(partners, peers):
    barrier = pltpu.get_barrier_semaphore()
    for peer in peers:
        pl.semaphore_signal(barrier, inc=1, device_id={"head": peer}, device_id_type=MESH)
    for exists, seq in partners:

        @pl.when(exists)
        def _():
            pl.semaphore_signal(barrier, inc=1, device_id={"seq": seq}, device_id_type=MESH)

    count = sum(exists.astype(jnp.int32) for exists, _ in partners)
    pl.semaphore_wait(barrier, count + len(peers))


def remote(src, dst, sems, index, device):
    return pltpu.make_async_remote_copy(
        src_ref=src,
        dst_ref=dst,
        send_sem=sems[0].at[index],
        recv_sem=sems[1].at[index],
        device_id=device,
        device_id_type=MESH,
    )


def for_heads(heads, body):
    def step(n, carry):
        body(n)
        return carry

    lax.fori_loop(0, heads, step, 0)


def gather_kernel(
    nh, q_in, k_in, v_in, g_in, q_out, g_out, kv_out, stage_buf, load, own, swap_s, swap_r, near_s, near_r
):
    heads, _, _, _, tile, _ = kv_out.shape
    rows = q_in.shape[0]
    h = lax.axis_index("head")
    partners = neighbours()
    up, down, before, after = partners
    peers = [lax.rem(h + j, nh) for j in range(1, nh)]
    senders = [lax.rem(h + nh - j, nh) for j in range(1, nh)]
    sources = (k_in, v_in, q_in, g_in)
    far_exists, far = far_row()
    share = nh // 2

    def place(array, n, owner):
        if array < 2:
            offset = pl.multiple_of(lax.rem(owner, share) * rows, rows)
            return kv_out.at[n, array, 1, 1 + lax.div(owner, share), pl.ds(offset, rows)]
        out = q_out if array == 2 else g_out
        return out.at[n, pl.ds(pl.multiple_of(owner * rows, rows), rows)]

    def columns(array, n, owner):
        start = pl.multiple_of((owner * heads + n) * HD, HD)
        return sources[array].at[:, pl.ds(start, HD)]

    def staged(array, n, owner):
        return stage_buf.at[array, owner * heads + n]

    def loaded(array, n, owner):
        return pltpu.make_async_copy(
            columns(array, n, owner), staged(array, n, owner), load.at[array, owner * heads + n]
        )

    def kept(array, n):
        return pltpu.make_async_copy(staged(array, n, h), place(array, n, h), own.at[array, n])

    def swapped(array, n, j, owner):
        return remote(
            staged(array, n, peers[j]),
            place(array, n, owner),
            (swap_s, swap_r),
            (array, j, n),
            {"head": peers[j]},
        )

    def start_load(arrays, n):
        for array in arrays:
            for owner in peers + [h]:
                loaded(array, n, owner).start()

    def start_swap(arrays, n):
        for array in arrays:
            for j in range(nh - 1):
                loaded(array, n, peers[j]).wait()
                swapped(array, n, j, h).start()
            loaded(array, n, h).wait()
            kept(array, n).start()

    def wait_swap(arrays, n):
        for array in arrays:
            for j in range(nh - 1):
                swapped(array, n, j, senders[j]).wait_recv()
            kept(array, n).wait()

    def block(n, row, first, count):
        return kv_out.at[n, :, row, pl.ds(first, count)]

    def copies(kind, n):
        if kind == 0:
            mine, plan = (1, 1, 2), ((up, (2, 1, 2), (0, 1, 2)), (down, (0, 1, 2), (2, 1, 2)))
        elif kind == 1:
            plan = ((before, (1, 3, 1), (1, 0, 1)), (after, (1, 0, 1), (1, 3, 1)))
        else:
            time = 0 if kind == 2 else 3
            plan = ((up, (2, time, 1), (0, time, 1)), (down, (0, time, 1), (2, time, 1)))
        found = []
        for side, (partner, there, here) in enumerate(plan):
            exists = partner[0]
            if kind == 2:
                exists = jnp.logical_and(exists, far != 2 * side)
            if kind == 1:
                mine = (1, 1 + side, 1)
            elif kind > 1:
                mine = (1, time, 1)
            device = {"seq": partner[1]}
            send = functools.partial(
                remote,
                block(n, *mine), block(n, *there), (near_s, near_r), (kind, side, n), device
            )
            arrive = functools.partial(
                remote,
                block(n, *mine), block(n, *here), (near_s, near_r), (kind, 1 - side, n), device
            )
            found.append((exists, send, arrive))
        return found

    def diagonal(n):
        device = {"seq": after[1]}
        return remote(
            block(n, far, 2, 1), block(n, far, 0, 1), (near_s, near_r), (4, 0, n), device
        )

    sends_diagonal = jnp.logical_and(after[0], far_exists)
    gets_diagonal = jnp.logical_and(before[0], far_exists)

    def each(kind, n, act):
        for exists, send, arrive in copies(kind, n):

            @pl.when(exists)
            def _():
                act(send, arrive)

    def start(send, arrive):
        send().start()

    for_heads(heads, lambda n: start_load((0, 1), n))
    for_heads(heads, lambda n: start_load((2, 3), n))
    greet(partners, peers)
    ahead = min(3, heads)
    for_heads(ahead, lambda n: start_swap((0, 1), n))

    def forward(n):
        each(0, n, lambda send, arrive: arrive().wait_recv())

        @pl.when(sends_diagonal)
        def _():
            diagonal(n).start()

        for exists_side, kind in ((0, 2), (1, 3)):
            exists, _, arrive = copies(1, n)[exists_side]

            @pl.when(exists)
            def _():
                arrive().wait_recv()
                each(kind, n, start)

    def stage(n):
        wait_swap((0, 1), n)
        each(0, n, start)
        each(1, n, start)

        @pl.when(n + ahead < heads)
        def _():
            start_swap((0, 1), n + ahead)

        @pl.when(n + ahead >= heads)
        def _():
            start_swap((2, 3), n + ahead - heads)

        @pl.when(n >= lag)
        def _():
            forward(n - lag)

    lag = min(2, heads)
    for_heads(heads, stage)
    for_heads(heads - ahead, lambda n: start_swap((2, 3), ahead + n))
    for_heads(lag, lambda n: forward(heads - lag + n))

    def finish(n):
        wait_swap((2, 3), n)
        for array in range(4):
            for j in range(nh - 1):
                swapped(array, n, j, h).wait_send()
        each(0, n, lambda send, arrive: send().wait_send())
        each(1, n, lambda send, arrive: send().wait_send())

        @pl.when(sends_diagonal)
        def _():
            diagonal(n).wait_send()

        @pl.when(gets_diagonal)
        def _():
            diagonal(n).wait_recv()

        for partner, kind in ((before, 2), (after, 3)):

            @pl.when(partner[0])
            def _():
                each(kind, n, lambda send, arrive: (send().wait_send(), arrive().wait_recv()))

    for_heads(heads, finish)


def exchange_in(queries, keys, values, out_grad):
    nh = lax.axis_size("head")
    rows, width = queries.shape
    heads, tile = width // HD // nh, rows * nh // 2
    dma = pltpu.SemaphoreType.DMA
    return pl.pallas_call(
        functools.partial(gather_kernel, nh),
        in_specs=[pl.BlockSpec(memory_space=pl.ANY)] * 4,
        out_specs=[pl.BlockSpec(memory_space=pl.ANY)] * 3,
        out_shape=[
            jax.ShapeDtypeStruct((heads, 2 * tile, HD), jnp.bfloat16),
            jax.ShapeDtypeStruct((heads, 2 * tile, HD), jnp.bfloat16),
            jax.ShapeDtypeStruct((heads, 2, 3, 4, tile, HD), jnp.bfloat16),
        ],
        scratch_shapes=[
            pltpu.VMEM((4, nh * heads, rows, HD), jnp.bfloat16),
            dma((4, nh * heads)),
            dma((4, heads)),
            dma((4, nh - 1, heads)),
            dma((4, nh - 1, heads)),
            dma((5, 2, heads)),
            dma((5, 2, heads)),
        ],
        compiler_params=pltpu.CompilerParams(
            collective_id=0, has_side_effects=True, vmem_limit_bytes=44 * 2**20
        ),
        name="gather",
    )(queries, keys, values, out_grad)


def scatter_kernel(
    nh,
    dq_in,
    dkv_in,
    dq_out,
    dk_out,
    dv_out,
    mine,
    sides,
    edges,
    times,
    final,
    landed,
    crossed,
    merged,
    load,
    load_far,
    pull,
    push,
    swap_s,
    swap_r,
    near_s,
    near_r,
):
    heads, _, _, _, tile, _ = dkv_in.shape
    rows = dq_out.shape[0]
    h = lax.axis_index("head")
    partners = neighbours()
    up, down, before, after = partners
    peers = [lax.rem(h + j, nh) for j in range(1, nh)]
    senders = [lax.rem(h + nh - j, nh) for j in range(1, nh)]
    outs = (dk_out, dv_out, dq_out)
    far_exists, far = far_row()
    far_side = lax.div(far, 2)
    sends_cross = jnp.logical_and(before[0], far_exists)
    gets_cross = jnp.logical_and(after[0], far_exists)

    def part(array, n, owner):
        span = pl.ds(pl.multiple_of(owner * rows, rows), rows)
        return dq_in.at[n, span] if array == 2 else final.at[n, array, span]

    def columns(array, n, owner):
        start = pl.multiple_of((owner * heads + n) * HD, HD)
        return outs[array].at[:, pl.ds(start, HD)]

    def pulled(n):
        return pltpu.make_async_copy(part(2, n, h), landed.at[2, h * heads + n], pull.at[n])

    def stored(array, n, owner):
        place = owner * heads + n
        src = landed.at[array, place]
        if array < 2 and owner is h:
            src = part(array, n, h)
        return pltpu.make_async_copy(src, columns(array, n, owner), push.at[array, place])

    def swapped(array, n, j, owner):
        return remote(
            part(array, n, peers[j]),
            landed.at[array, owner * heads + n],
            (swap_s, swap_r),
            (array, j, n),
            {"head": peers[j]},
        )

    def start_swap(arrays, n):
        for array in arrays:
            for j in range(nh - 1):
                swapped(array, n, j, h).start()
            if array == 2:
                pulled(n).start()
            else:
                stored(array, n, h).start()

    def settle(arrays, n):
        for array in arrays:
            if array == 2:
                pulled(n).wait()
                stored(array, n, h).start()
            for j in range(nh - 1):
                swapped(array, n, j, senders[j]).wait_recv()
                stored(array, n, senders[j]).start()

    def copies(kind, n):
        if kind == 0:
            plan = ((up, 0), (down, 1))
        else:
            plan = ((before, 0), (after, 1))
        found = []
        for partner, side in plan:
            exists = partner[0]
            if kind == 0:
                exists = jnp.logical_and(exists, far_side != side)
                src, dst, here = dkv_in.at[n, :, 2 * side], sides.at[n, 1 - side], sides.at[n, side]
            else:
                src, dst, here = edges.at[n, side], times.at[n, 1 - side], times.at[n, side]
            device = {"seq": partner[1]}
            send = functools.partial(
                remote, src, dst, (near_s, near_r), (kind, side, n), device)
            arrive = functools.partial(
                remote, src, here, (near_s, near_r), (kind, 1 - side, n), device)
            found.append((exists, send, arrive))
        return found

    def each(kind, n, act):
        for exists, send, arrive in copies(kind, n):

            @pl.when(exists)
            def _():
                act(send, arrive)

    def loaded(n):
        return pltpu.make_async_copy(dkv_in.at[n, :, 1], mine.at[n], load.at[n])

    def loaded_far(n):
        return pltpu.make_async_copy(dkv_in.at[n, :, far, 2], merged.at[n], load_far.at[n])

    def across(n, k, side):
        time = (1, 3, 2)[k]
        src = merged.at[n] if k == 2 else dkv_in.at[n, :, far, time]
        device = {"seq": lax.axis_index("seq") + far - 1}
        index = (2 + k // 2, k % 2, n)
        return remote(src, sides.at[n, side, :, time], (near_s, near_r), index, device)

    def cross(n):
        device = {"seq": before[1]}
        return remote(
            dkv_in.at[n, :, far, 0], crossed.at[n], (near_s, near_r), (3, 1, n), device
        )

    greet(partners, peers)

    def begin(n):
        @pl.when(sends_cross)
        def _():
            cross(n).start()

        each(0, n, lambda send, arrive: send().start())
        loaded(n).start()

        @pl.when(far_exists)
        def _():
            loaded_far(n).start()
            across(n, 0, 1 - far_side).start()
            across(n, 1, 1 - far_side).start()

    def merge(n):
        @pl.when(far_exists)
        def _():
            loaded_far(n).wait()

        @pl.when(gets_cross)
        def _():
            cross(n).wait_recv()
            total = merged[n].astype(jnp.float32) + crossed[n].astype(jnp.float32)
            merged[n] = total.astype(jnp.bfloat16)

        @pl.when(far_exists)
        def _():
            across(n, 2, 1 - far_side).start()

    ahead = min(4, heads)
    for_heads(ahead, begin)
    for_heads(heads, lambda n: start_swap((2,), n))
    for buffer, pair in ((sides, (up, down)), (times, (before, after))):
        for side, partner in enumerate(pair):

            @pl.when(jnp.logical_not(partner[0]))
            def _():
                def clear(n):
                    buffer[n, side] = jnp.zeros(buffer.shape[2:], buffer.dtype)

                for_heads(heads, clear)

    def clear_far(n):
        sides[n, far_side, :, 0] = jnp.zeros(merged.shape[1:], merged.dtype)

    for_heads(heads, clear_far)

    def column(n, which, time):
        terms = (mine[n, which, time], sides[n, 0, which, time], sides[n, 1, which, time])
        first, second, third = (term.astype(jnp.float32) for term in terms)
        return first + second + third

    def wrap_up(n):
        each(1, n, lambda send, arrive: arrive().wait_recv())
        for which in range(2):
            for place in range(2):
                total = column(n, which, 1 + place) + times[n, place, which].astype(jnp.float32)
                final[n, which, pl.ds(place * tile, tile)] = total.astype(jnp.bfloat16)
        start_swap((0, 1), n)
        settle((2,), n)

        @pl.when(n >= lag)
        def _():
            settle((0, 1), n - lag)

    lag = min(2, heads)

    def stage(n):
        each(0, n, lambda send, arrive: arrive().wait_recv())
        loaded(n).wait()

        @pl.when(far_exists)
        def _():
            for k in range(3):
                across(n, k, far_side).wait_recv()

        for which in range(2):
            for side in range(2):
                edges[n, side, which] = column(n, which, 3 * side).astype(jnp.bfloat16)
        each(1, n, lambda send, arrive: send().start())

    def step(n):
        merge(n)

        @pl.when(n + ahead < heads)
        def _():
            begin(n + ahead)

        @pl.when(n >= 1)
        def _():
            stage(n - 1)

        @pl.when(n >= 2)
        def _():
            wrap_up(n - 2)

    for_heads(heads, step)
    stage(heads - 1)
    for_heads(lag, lambda n: wrap_up(heads - lag + n))
    for_heads(lag, lambda n: settle((0, 1), heads - lag + n))

    def finish(n):
        for array in range(3):
            for j in range(nh - 1):
                swapped(array, n, j, h).wait_send()
                stored(array, n, senders[j]).wait()
            stored(array, n, h).wait()
        each(0, n, lambda send, arrive: send().wait_send())
        each(1, n, lambda send, arrive: send().wait_send())

        @pl.when(sends_cross)
        def _():
            cross(n).wait_send()

        @pl.when(far_exists)
        def _():
            for k in range(3):
                across(n, k, 1 - far_side).wait_send()

    for_heads(heads, finish)


def exchange_out(dq, dkv):
    nh = lax.axis_size("head")
    heads, rows, _ = dq.shape
    tile = rows // 2
    dma = pltpu.SemaphoreType.DMA
    whole = jax.ShapeDtypeStruct((rows // nh, nh * heads * HD), jnp.bfloat16)

    def held(*shape):
        return pltpu.VMEM(shape + (HD,), jnp.bfloat16)

    return pl.pallas_call(
        functools.partial(scatter_kernel, nh),
        in_specs=[pl.BlockSpec(memory_space=pl.ANY)] * 2,
        out_specs=[pl.BlockSpec(memory_space=pl.ANY)] * 3,
        out_shape=[whole] * 3,
        scratch_shapes=[
            held(heads, 2, 4, tile),
            held(heads, 2, 2, 4, tile),
            held(heads, 2, 2, tile),
            held(heads, 2, 2, tile),
            held(heads, 2, 2 * tile),
            held(3, nh * heads, rows // nh),
            held(heads, 2, tile),
            held(heads, 2, tile),
            dma((heads,)),
            dma((heads,)),
            dma((heads,)),
            dma((3, nh * heads)),
            dma((3, nh - 1, heads)),
            dma((3, nh - 1, heads)),
            dma((4, 2, heads)),
            dma((4, 2, heads)),
        ],
        compiler_params=pltpu.CompilerParams(
            collective_id=1, has_side_effects=True, vmem_limit_bytes=44 * 2**20
        ),
        name="scatter",
    )(dq, dkv)


def per_device(queries, keys, values, out_grad, window):
    q, g, kv = exchange_in(queries, keys, values, out_grad)
    dq, dkv = attend(visible_slots(window, q.shape[0]), q, g, kv)
    return exchange_out(dq, dkv)


def solution(mesh):
    rows = P(("seq", "head"), None)
    return jax.shard_map(
        per_device,
        mesh=mesh,
        in_specs=(rows, rows, rows, rows, P()),
        out_specs=(rows, rows, rows),
        check_vma=False,
    )
```

```python
import functools

import jax
import jax.numpy as jnp
from jax import lax
from jax.experimental import pallas as pl
from jax.experimental.pallas import tpu as pltpu
from jax.sharding import PartitionSpec as P

HD = 128
GH = 4
SCALE = HD ** (-0.5)
LOG2E = 1.4426950408889634
MESH = pl.DeviceIdType.MESH


def visible_slots(window, heads_here):
    seq_index = lax.axis_index("seq")
    grid_time = 2 * (lax.axis_size("seq") // GH)
    reaches = lax.dynamic_slice_in_dim(window, lax.axis_index("head") * heads_here, heads_here, 0)
    slot = jnp.arange(9)
    time_off, row_off = slot // 3 - 1, slot % 3 - 1
    near_time = 2 * (seq_index // GH) + jnp.arange(2)[:, None] + time_off[None, :]
    near_row = seq_index % GH + row_off
    inside = (near_time >= 0) & (near_time < grid_time)
    inside = inside & ((near_row >= 0) & (near_row < GH))[None, :]
    reach = (jnp.abs(time_off)[None, :] <= reaches[:, :1]) & (
        jnp.abs(row_off)[None, :] <= reaches[:, 1:]
    )
    return (inside[None] & reach[:, None, :]).astype(jnp.int32).reshape(-1)


def dot(a, b, dims):
    return lax.dot_general(a, b, (dims, ((), ())), preferred_element_type=jnp.float32)


def attend_kernel(
    vis_ref, q_ref, g_ref, kv_ref, dq_ref, dkv_ref, e_scr, dp_scr, acc, dqt, tops, top, total, delta
):
    head = pl.program_id(0)
    tile = q_ref.shape[1] // 2

    def seen(qt, row, time):
        step = time - qt
        inside = jnp.logical_and(step >= 0, step < 3)
        slot = jnp.clip(step, 0, 2) * 3 + row
        return jnp.logical_and(inside, vis_ref[(head * 2 + qt) * 9 + slot] == 1)

    def one_tile(qt, carry):
        rows = pl.ds(pl.multiple_of(qt * tile, tile), tile)
        q = q_ref[0, rows, :]
        g = g_ref[0, rows, :]
        top[...] = jnp.full_like(top, -jnp.inf)
        total[...] = jnp.zeros_like(total)
        delta[...] = jnp.zeros_like(delta)
        dqt[...] = jnp.zeros_like(dqt)

        def over_visible(body):
            def by_row(row, carry):
                first = (head * 2 + qt) * 9 + row
                parts = [vis_ref[first + 3 * step] for step in range(3)]
                full = parts[0] + parts[1] + parts[2] == 3

                @pl.when(full)
                def _():
                    body(row * 3, row, qt, 3)

                @pl.when(jnp.logical_not(full))
                def _():
                    def single(step, carry):
                        @pl.when(vis_ref[first + 3 * step] == 1)
                        def _():
                            body(row * 3 + step, row, qt + step, 1)

                        return carry

                    lax.fori_loop(0, 3, single, 0)

                return carry

            lax.fori_loop(0, 3, by_row, 0)

        def near(which, row, time, span):
            return kv_ref[0, which, row, pl.ds(time, span)].reshape(span * tile, HD)

        def scores(slot, row, time, span):
            s = dot(near(0, row, time, span), q, ((1,), (1,)))
            old = top[...]
            new = jnp.maximum(old, jnp.max(s, axis=0, keepdims=True))
            shrink = jnp.exp2((old - new) * (SCALE * LOG2E))
            dp = dot(near(1, row, time, span), g, ((1,), (1,)))
            e = jnp.exp2((s - new) * (SCALE * LOG2E))
            e_scr[pl.ds(slot, span)] = e.reshape(span, tile, tile)
            dp_scr[pl.ds(slot, span)] = dp.reshape(span, tile, tile)
            tops[slot] = new
            top[...] = new
            total[...] = total[...] * shrink + jnp.sum(e, axis=0, keepdims=True)
            delta[...] = delta[...] * shrink + jnp.sum(e * dp, axis=0, keepdims=True)

        def grads(slot, row, time, span):
            for step in range(span):

                @pl.when(jnp.logical_or(qt == 0, jnp.logical_not(seen(0, row, time + step))))
                def _():
                    acc[:, row, time + step] = jnp.zeros((2,) + acc.shape[3:], jnp.float32)

            def flat(ref):
                return ref[pl.ds(slot, span)].reshape(span * tile, tile)

            times = pl.ds(time, span)
            shape = (span, tile, HD)
            p = flat(e_scr) * (jnp.exp2((tops[slot] - top[...]) * (SCALE * LOG2E)) * total[...])
            ds = (p * (flat(dp_scr) - delta[...])).astype(jnp.bfloat16)
            acc[1, row, times] += dot(p.astype(jnp.bfloat16), g, ((1,), (0,))).reshape(shape)
            acc[0, row, times] += dot(ds, q, ((1,), (0,))).reshape(shape)
            dqt[...] += dot(near(0, row, time, span), ds, ((0,), (0,)))

        over_visible(scores)
        total[...] = 1.0 / total[...]
        delta[...] = delta[...] * total[...]
        over_visible(grads)
        dq_ref[0, rows, :] = (dqt[...] * SCALE).T.astype(jnp.bfloat16)
        return carry

    lax.fori_loop(0, 2, one_tile, 0)

    def hand_out(index, carry):
        row, time = lax.div(index, 4), lax.rem(index, 4)
        used = jnp.logical_or(seen(0, row, time), seen(1, row, time))

        @pl.when(used)
        def _():
            dkv_ref[0, 0, row, time] = (acc[0, row, time] * SCALE).astype(jnp.bfloat16)
            dkv_ref[0, 1, row, time] = acc[1, row, time].astype(jnp.bfloat16)

        @pl.when(jnp.logical_not(used))
        def _():
            dkv_ref[0, :, row, time] = jnp.zeros((2,) + acc.shape[3:], jnp.bfloat16)

        return carry

    lax.fori_loop(0, 12, hand_out, 0)


def attend(vis, q, g, kv):
    heads, rows, _ = q.shape
    tile = rows // 2
    by_head = lambda shape: pl.BlockSpec(
        (1,) + shape, lambda n, vis: (n,) + (0,) * len(shape)
    )
    pairs = heads * 18
    return pl.pallas_call(
        attend_kernel,
        grid_spec=pltpu.PrefetchScalarGridSpec(
            num_scalar_prefetch=1,
            grid=(heads,),
            in_specs=[
                by_head((rows, HD)),
                by_head((rows, HD)),
                by_head((2, 3, 4, tile, HD)),
            ],
            out_specs=[by_head((rows, HD)), by_head((2, 3, 4, tile, HD))],
            scratch_shapes=[
                pltpu.VMEM((9, tile, tile), jnp.float32),
                pltpu.VMEM((9, tile, tile), jnp.float32),
                pltpu.VMEM((2, 3, 4, tile, HD), jnp.float32),
                pltpu.VMEM((HD, tile), jnp.float32),
                pltpu.VMEM((9, 1, tile), jnp.float32),
                pltpu.VMEM((1, tile), jnp.float32),
                pltpu.VMEM((1, tile), jnp.float32),
                pltpu.VMEM((1, tile), jnp.float32),
            ],
        ),
        out_shape=[
            jax.ShapeDtypeStruct(q.shape, jnp.bfloat16),
            jax.ShapeDtypeStruct(kv.shape, jnp.bfloat16),
        ],
        compiler_params=pltpu.CompilerParams(
            dimension_semantics=("arbitrary",), vmem_limit_bytes=48 * 2**20
        ),
        cost_estimate=pl.CostEstimate(
            flops=pairs * 5 * tile * tile * HD,
            bytes_accessed=4 * kv.size + 6 * q.size,
            transcendentals=pairs * tile * tile // 2,
        ),
        name="attend",
    )(vis, q, g, kv)


def neighbours():
    seq = lax.axis_index("seq")
    row, slab = lax.rem(seq, GH), lax.div(seq, GH)
    slabs = lax.axis_size("seq") // GH
    return (
        (row > 0, seq - 1),
        (row < GH - 1, seq + 1),
        (slab > 0, seq - GH),
        (slab < slabs - 1, seq + GH),
    )


def far_row():
    row = lax.rem(lax.axis_index("seq"), GH)
    odd = lax.rem(row, 2)
    exists = jnp.where(odd == 1, row < GH - 1, row > 0)
    return exists, 2 * odd


def greet(partners, peers):
    barrier = pltpu.get_barrier_semaphore()
    for peer in peers:
        pl.semaphore_signal(barrier, inc=1, device_id={"head": peer}, device_id_type=MESH)
    for exists, seq in partners:

        @pl.when(exists)
        def _():
            pl.semaphore_signal(barrier, inc=1, device_id={"seq": seq}, device_id_type=MESH)

    count = sum(exists.astype(jnp.int32) for exists, _ in partners)
    pl.semaphore_wait(barrier, count + len(peers))


def remote(src, dst, sems, index, device):
    return pltpu.make_async_remote_copy(
        src_ref=src,
        dst_ref=dst,
        send_sem=sems[0].at[index],
        recv_sem=sems[1].at[index],
        device_id=device,
        device_id_type=MESH,
    )


def for_heads(heads, body):
    def step(n, carry):
        body(n)
        return carry

    lax.fori_loop(0, heads, step, 0)


def gather_kernel(
    nh, q_in, k_in, v_in, g_in, q_out, g_out, kv_out, stage_buf, load, own, swap_s, swap_r, near_s, near_r
):
    heads, _, _, _, tile, _ = kv_out.shape
    rows = q_in.shape[0]
    h = lax.axis_index("head")
    partners = neighbours()
    up, down, before, after = partners
    peers = [lax.rem(h + j, nh) for j in range(1, nh)]
    senders = [lax.rem(h + nh - j, nh) for j in range(1, nh)]
    sources = (k_in, v_in, q_in, g_in)
    far_exists, far = far_row()
    share = nh // 2

    def place(array, n, owner):
        if array < 2:
            offset = pl.multiple_of(lax.rem(owner, share) * rows, rows)
            return kv_out.at[n, array, 1, 1 + lax.div(owner, share), pl.ds(offset, rows)]
        out = q_out if array == 2 else g_out
        return out.at[n, pl.ds(pl.multiple_of(owner * rows, rows), rows)]

    def columns(array, n, owner):
        start = pl.multiple_of((owner * heads + n) * HD, HD)
        return sources[array].at[:, pl.ds(start, HD)]

    def staged(array, n, owner):
        return stage_buf.at[array, owner * heads + n]

    def loaded(array, n, owner):
        return pltpu.make_async_copy(
            columns(array, n, owner), staged(array, n, owner), load.at[array, owner * heads + n]
        )

    def kept(array, n):
        return pltpu.make_async_copy(staged(array, n, h), place(array, n, h), own.at[array, n])

    def swapped(array, n, j, owner):
        return remote(
            staged(array, n, peers[j]),
            place(array, n, owner),
            (swap_s, swap_r),
            (array, j, n),
            {"head": peers[j]},
        )

    def start_load(arrays, n):
        for array in arrays:
            for owner in peers + [h]:
                loaded(array, n, owner).start()

    def start_swap(arrays, n):
        for array in arrays:
            for j in range(nh - 1):
                loaded(array, n, peers[j]).wait()
                swapped(array, n, j, h).start()
            loaded(array, n, h).wait()
            kept(array, n).start()

    def wait_swap(arrays, n):
        for array in arrays:
            for j in range(nh - 1):
                swapped(array, n, j, senders[j]).wait_recv()
            kept(array, n).wait()

    def block(n, row, first, count):
        return kv_out.at[n, :, row, pl.ds(first, count)]

    def copies(kind, n):
        if kind == 0:
            mine, plan = (1, 1, 2), ((up, (2, 1, 2), (0, 1, 2)), (down, (0, 1, 2), (2, 1, 2)))
        elif kind == 1:
            plan = ((before, (1, 3, 1), (1, 0, 1)), (after, (1, 0, 1), (1, 3, 1)))
        else:
            time = 0 if kind == 2 else 3
            plan = ((up, (2, time, 1), (0, time, 1)), (down, (0, time, 1), (2, time, 1)))
        found = []
        for side, (partner, there, here) in enumerate(plan):
            exists = partner[0]
            if kind == 2:
                exists = jnp.logical_and(exists, far != 2 * side)
            if kind == 1:
                mine = (1, 1 + side, 1)
            elif kind > 1:
                mine = (1, time, 1)
            device = {"seq": partner[1]}
            send = functools.partial(
                remote,
                block(n, *mine), block(n, *there), (near_s, near_r), (kind, side, n), device
            )
            arrive = functools.partial(
                remote,
                block(n, *mine), block(n, *here), (near_s, near_r), (kind, 1 - side, n), device
            )
            found.append((exists, send, arrive))
        return found

    def diagonal(n):
        device = {"seq": after[1]}
        return remote(
            block(n, far, 2, 1), block(n, far, 0, 1), (near_s, near_r), (4, 0, n), device
        )

    sends_diagonal = jnp.logical_and(after[0], far_exists)
    gets_diagonal = jnp.logical_and(before[0], far_exists)

    def each(kind, n, act):
        for exists, send, arrive in copies(kind, n):

            @pl.when(exists)
            def _():
                act(send, arrive)

    def start(send, arrive):
        send().start()

    for_heads(heads, lambda n: start_load((0, 1), n))
    for_heads(heads, lambda n: start_load((2, 3), n))
    greet(partners, peers)
    ahead = min(3, heads)
    for_heads(ahead, lambda n: start_swap((0, 1), n))

    def forward(n):
        each(0, n, lambda send, arrive: arrive().wait_recv())

        @pl.when(sends_diagonal)
        def _():
            diagonal(n).start()

        for exists_side, kind in ((0, 2), (1, 3)):
            exists, _, arrive = copies(1, n)[exists_side]

            @pl.when(exists)
            def _():
                arrive().wait_recv()
                each(kind, n, start)

    def stage(n):
        wait_swap((0, 1), n)
        each(0, n, start)
        each(1, n, start)

        @pl.when(n + ahead < heads)
        def _():
            start_swap((0, 1), n + ahead)

        @pl.when(n + ahead >= heads)
        def _():
            start_swap((2, 3), n + ahead - heads)

        @pl.when(n >= lag)
        def _():
            forward(n - lag)

    lag = min(2, heads)
    for_heads(heads, stage)
    for_heads(heads - ahead, lambda n: start_swap((2, 3), ahead + n))
    for_heads(lag, lambda n: forward(heads - lag + n))

    def finish(n):
        wait_swap((2, 3), n)
        for array in range(4):
            for j in range(nh - 1):
                swapped(array, n, j, h).wait_send()
        each(0, n, lambda send, arrive: send().wait_send())
        each(1, n, lambda send, arrive: send().wait_send())

        @pl.when(sends_diagonal)
        def _():
            diagonal(n).wait_send()

        @pl.when(gets_diagonal)
        def _():
            diagonal(n).wait_recv()

        for partner, kind in ((before, 2), (after, 3)):

            @pl.when(partner[0])
            def _():
                each(kind, n, lambda send, arrive: (send().wait_send(), arrive().wait_recv()))

    for_heads(heads, finish)


def exchange_in(queries, keys, values, out_grad):
    nh = lax.axis_size("head")
    rows, width = queries.shape
    heads, tile = width // HD // nh, rows * nh // 2
    dma = pltpu.SemaphoreType.DMA
    return pl.pallas_call(
        functools.partial(gather_kernel, nh),
        in_specs=[pl.BlockSpec(memory_space=pl.ANY)] * 4,
        out_specs=[pl.BlockSpec(memory_space=pl.ANY)] * 3,
        out_shape=[
            jax.ShapeDtypeStruct((heads, 2 * tile, HD), jnp.bfloat16),
            jax.ShapeDtypeStruct((heads, 2 * tile, HD), jnp.bfloat16),
            jax.ShapeDtypeStruct((heads, 2, 3, 4, tile, HD), jnp.bfloat16),
        ],
        scratch_shapes=[
            pltpu.VMEM((4, nh * heads, rows, HD), jnp.bfloat16),
            dma((4, nh * heads)),
            dma((4, heads)),
            dma((4, nh - 1, heads)),
            dma((4, nh - 1, heads)),
            dma((5, 2, heads)),
            dma((5, 2, heads)),
        ],
        compiler_params=pltpu.CompilerParams(
            collective_id=0, has_side_effects=True, vmem_limit_bytes=44 * 2**20
        ),
        name="gather",
    )(queries, keys, values, out_grad)


def scatter_kernel(
    nh,
    dq_in,
    dkv_in,
    dq_out,
    dk_out,
    dv_out,
    mine,
    sides,
    edges,
    times,
    final,
    landed,
    crossed,
    merged,
    load,
    load_far,
    pull,
    push,
    swap_s,
    swap_r,
    near_s,
    near_r,
):
    heads, _, _, _, tile, _ = dkv_in.shape
    rows = dq_out.shape[0]
    h = lax.axis_index("head")
    partners = neighbours()
    up, down, before, after = partners
    peers = [lax.rem(h + j, nh) for j in range(1, nh)]
    senders = [lax.rem(h + nh - j, nh) for j in range(1, nh)]
    outs = (dk_out, dv_out, dq_out)
    far_exists, far = far_row()
    far_side = lax.div(far, 2)
    sends_cross = jnp.logical_and(before[0], far_exists)
    gets_cross = jnp.logical_and(after[0], far_exists)

    def part(array, n, owner):
        span = pl.ds(pl.multiple_of(owner * rows, rows), rows)
        return dq_in.at[n, span] if array == 2 else final.at[n, array, span]

    def columns(array, n, owner):
        start = pl.multiple_of((owner * heads + n) * HD, HD)
        return outs[array].at[:, pl.ds(start, HD)]

    def pulled(n):
        return pltpu.make_async_copy(part(2, n, h), landed.at[2, h * heads + n], pull.at[n])

    def stored(array, n, owner):
        place = owner * heads + n
        src = landed.at[array, place]
        if array < 2 and owner is h:
            src = part(array, n, h)
        return pltpu.make_async_copy(src, columns(array, n, owner), push.at[array, place])

    def swapped(array, n, j, owner):
        return remote(
            part(array, n, peers[j]),
            landed.at[array, owner * heads + n],
            (swap_s, swap_r),
            (array, j, n),
            {"head": peers[j]},
        )

    def start_swap(arrays, n):
        for array in arrays:
            for j in range(nh - 1):
                swapped(array, n, j, h).start()
            if array == 2:
                pulled(n).start()
            else:
                stored(array, n, h).start()

    def settle(arrays, n):
        for array in arrays:
            if array == 2:
                pulled(n).wait()
                stored(array, n, h).start()
            for j in range(nh - 1):
                swapped(array, n, j, senders[j]).wait_recv()
                stored(array, n, senders[j]).start()

    def copies(kind, n):
        if kind == 0:
            plan = ((up, 0), (down, 1))
        else:
            plan = ((before, 0), (after, 1))
        found = []
        for partner, side in plan:
            exists = partner[0]
            if kind == 0:
                exists = jnp.logical_and(exists, far_side != side)
                src, dst, here = dkv_in.at[n, :, 2 * side], sides.at[n, 1 - side], sides.at[n, side]
            else:
                src, dst, here = edges.at[n, side], times.at[n, 1 - side], times.at[n, side]
            device = {"seq": partner[1]}
            send = functools.partial(
                remote, src, dst, (near_s, near_r), (kind, side, n), device)
            arrive = functools.partial(
                remote, src, here, (near_s, near_r), (kind, 1 - side, n), device)
            found.append((exists, send, arrive))
        return found

    def each(kind, n, act):
        for exists, send, arrive in copies(kind, n):

            @pl.when(exists)
            def _():
                act(send, arrive)

    def loaded(n):
        return pltpu.make_async_copy(dkv_in.at[n, :, 1], mine.at[n], load.at[n])

    def loaded_far(n):
        return pltpu.make_async_copy(dkv_in.at[n, :, far, 2], merged.at[n], load_far.at[n])

    def across(n, k, side):
        time = (1, 3, 2)[k]
        src = merged.at[n] if k == 2 else dkv_in.at[n, :, far, time]
        device = {"seq": lax.axis_index("seq") + far - 1}
        index = (2 + k // 2, k % 2, n)
        return remote(src, sides.at[n, side, :, time], (near_s, near_r), index, device)

    def cross(n):
        device = {"seq": before[1]}
        return remote(
            dkv_in.at[n, :, far, 0], crossed.at[n], (near_s, near_r), (3, 1, n), device
        )

    greet(partners, peers)

    def begin(n):
        @pl.when(sends_cross)
        def _():
            cross(n).start()

        each(0, n, lambda send, arrive: send().start())
        loaded(n).start()

        @pl.when(far_exists)
        def _():
            loaded_far(n).start()
            across(n, 0, 1 - far_side).start()
            across(n, 1, 1 - far_side).start()

    def merge(n):
        @pl.when(far_exists)
        def _():
            loaded_far(n).wait()

        @pl.when(gets_cross)
        def _():
            cross(n).wait_recv()
            total = merged[n].astype(jnp.float32) + crossed[n].astype(jnp.float32)
            merged[n] = total.astype(jnp.bfloat16)

        @pl.when(far_exists)
        def _():
            across(n, 2, 1 - far_side).start()

    ahead = min(4, heads)
    for_heads(ahead, begin)
    for_heads(heads, lambda n: start_swap((2,), n))
    for buffer, pair in ((sides, (up, down)), (times, (before, after))):
        for side, partner in enumerate(pair):

            @pl.when(jnp.logical_not(partner[0]))
            def _():
                def clear(n):
                    buffer[n, side] = jnp.zeros(buffer.shape[2:], buffer.dtype)

                for_heads(heads, clear)

    def clear_far(n):
        sides[n, far_side, :, 0] = jnp.zeros(merged.shape[1:], merged.dtype)

    for_heads(heads, clear_far)

    def column(n, which, time):
        terms = (mine[n, which, time], sides[n, 0, which, time], sides[n, 1, which, time])
        first, second, third = (term.astype(jnp.float32) for term in terms)
        return first + second + third

    def wrap_up(n):
        each(1, n, lambda send, arrive: arrive().wait_recv())
        for which in range(2):
            for place in range(2):
                total = column(n, which, 1 + place) + times[n, place, which].astype(jnp.float32)
                final[n, which, pl.ds(place * tile, tile)] = total.astype(jnp.bfloat16)
        start_swap((0, 1), n)
        settle((2,), n)

        @pl.when(n >= lag)
        def _():
            settle((0, 1), n - lag)

    lag = min(2, heads)

    def stage(n):
        each(0, n, lambda send, arrive: arrive().wait_recv())
        loaded(n).wait()

        @pl.when(far_exists)
        def _():
            for k in range(3):
                across(n, k, far_side).wait_recv()

        for which in range(2):
            for side in range(2):
                edges[n, side, which] = column(n, which, 3 * side).astype(jnp.bfloat16)
        each(1, n, lambda send, arrive: send().start())

    def step(n):
        merge(n)

        @pl.when(n + ahead < heads)
        def _():
            begin(n + ahead)

        @pl.when(n >= 1)
        def _():
            stage(n - 1)

        @pl.when(n >= 2)
        def _():
            wrap_up(n - 2)

    for_heads(heads, step)
    stage(heads - 1)
    for_heads(lag, lambda n: wrap_up(heads - lag + n))
    for_heads(lag, lambda n: settle((0, 1), heads - lag + n))

    def finish(n):
        for array in range(3):
            for j in range(nh - 1):
                swapped(array, n, j, h).wait_send()
                stored(array, n, senders[j]).wait()
            stored(array, n, h).wait()
        each(0, n, lambda send, arrive: send().wait_send())
        each(1, n, lambda send, arrive: send().wait_send())

        @pl.when(sends_cross)
        def _():
            cross(n).wait_send()

        @pl.when(far_exists)
        def _():
            for k in range(3):
                across(n, k, 1 - far_side).wait_send()

    for_heads(heads, finish)


def exchange_out(dq, dkv):
    nh = lax.axis_size("head")
    heads, rows, _ = dq.shape
    tile = rows // 2
    dma = pltpu.SemaphoreType.DMA
    whole = jax.ShapeDtypeStruct((rows // nh, nh * heads * HD), jnp.bfloat16)

    def held(*shape):
        return pltpu.VMEM(shape + (HD,), jnp.bfloat16)

    return pl.pallas_call(
        functools.partial(scatter_kernel, nh),
        in_specs=[pl.BlockSpec(memory_space=pl.ANY)] * 2,
        out_specs=[pl.BlockSpec(memory_space=pl.ANY)] * 3,
        out_shape=[whole] * 3,
        scratch_shapes=[
            held(heads, 2, 4, tile),
            held(heads, 2, 2, 4, tile),
            held(heads, 2, 2, tile),
            held(heads, 2, 2, tile),
            held(heads, 2, 2 * tile),
            held(3, nh * heads, rows // nh),
            held(heads, 2, tile),
            held(heads, 2, tile),
            dma((heads,)),
            dma((heads,)),
            dma((heads,)),
            dma((3, nh * heads)),
            dma((3, nh - 1, heads)),
            dma((3, nh - 1, heads)),
            dma((4, 2, heads)),
            dma((4, 2, heads)),
        ],
        compiler_params=pltpu.CompilerParams(
            collective_id=1, has_side_effects=True, vmem_limit_bytes=44 * 2**20
        ),
        name="scatter",
    )(dq, dkv)


def per_device(queries, keys, values, out_grad, window):
    q, g, kv = exchange_in(queries, keys, values, out_grad)
    dq, dkv = attend(visible_slots(window, q.shape[0]), q, g, kv)
    return exchange_out(dq, dkv)


def solution(mesh):
    rows = P(("seq", "head"), None)
    return jax.shard_map(
        per_device,
        mesh=mesh,
        in_specs=(rows, rows, rows, rows, P()),
        out_specs=(rows, rows, rows),
        check_vma=False,
    )
```

```python
import functools

import jax
import jax.numpy as jnp
from jax import lax
from jax.experimental import pallas as pl
from jax.experimental.pallas import tpu as pltpu
from jax.sharding import PartitionSpec as P

HD = 128
GH = 4
SCALE = HD ** (-0.5)
LOG2E = 1.4426950408889634
MESH = pl.DeviceIdType.MESH


def visible_slots(window, heads_here):
    seq_index = lax.axis_index("seq")
    grid_time = 2 * (lax.axis_size("seq") // GH)
    reaches = lax.dynamic_slice_in_dim(window, lax.axis_index("head") * heads_here, heads_here, 0)
    slot = jnp.arange(9)
    time_off, row_off = slot // 3 - 1, slot % 3 - 1
    near_time = 2 * (seq_index // GH) + jnp.arange(2)[:, None] + time_off[None, :]
    near_row = seq_index % GH + row_off
    inside = (near_time >= 0) & (near_time < grid_time)
    inside = inside & ((near_row >= 0) & (near_row < GH))[None, :]
    reach = (jnp.abs(time_off)[None, :] <= reaches[:, :1]) & (
        jnp.abs(row_off)[None, :] <= reaches[:, 1:]
    )
    return (inside[None] & reach[:, None, :]).astype(jnp.int32).reshape(-1)


def dot(a, b, dims):
    return lax.dot_general(a, b, (dims, ((), ())), preferred_element_type=jnp.float32)


def attend_kernel(
    vis_ref, q_ref, g_ref, kv_ref, dq_ref, dkv_ref, e_scr, dp_scr, acc, dqt, tops, top, total, delta
):
    head = pl.program_id(0)
    tile = q_ref.shape[1] // 2

    def seen(qt, row, time):
        step = time - qt
        inside = jnp.logical_and(step >= 0, step < 3)
        slot = jnp.clip(step, 0, 2) * 3 + row
        return jnp.logical_and(inside, vis_ref[(head * 2 + qt) * 9 + slot] == 1)

    def one_tile(qt, carry):
        rows = pl.ds(pl.multiple_of(qt * tile, tile), tile)
        q = q_ref[0, rows, :]
        g = g_ref[0, rows, :]
        q_cols, g_cols = q.T, g.T
        top[...] = jnp.full_like(top, -jnp.inf)
        total[...] = jnp.zeros_like(total)
        delta[...] = jnp.zeros_like(delta)
        dqt[...] = jnp.zeros_like(dqt)

        def over_visible(body):
            def by_row(row, carry):
                first = (head * 2 + qt) * 9 + row
                parts = [vis_ref[first + 3 * step] for step in range(3)]
                full = parts[0] + parts[1] + parts[2] == 3

                @pl.when(full)
                def _():
                    body(row * 3, row, qt, 3)

                @pl.when(jnp.logical_not(full))
                def _():
                    def single(step, carry):
                        @pl.when(vis_ref[first + 3 * step] == 1)
                        def _():
                            body(row * 3 + step, row, qt + step, 1)

                        return carry

                    lax.fori_loop(0, 3, single, 0)

                return carry

            lax.fori_loop(0, 3, by_row, 0)

        def near(which, row, time, span):
            return kv_ref[0, which, row, pl.ds(time, span)].reshape(span * tile, HD)

        def scores(slot, row, time, span):
            s = dot(near(0, row, time, span), q_cols, ((1,), (0,)))
            old = top[...]
            new = jnp.maximum(old, jnp.max(s, axis=0, keepdims=True))
            shrink = jnp.exp2((old - new) * (SCALE * LOG2E))
            dp = dot(near(1, row, time, span), g_cols, ((1,), (0,)))
            e = jnp.exp2((s - new) * (SCALE * LOG2E))
            e_scr[pl.ds(slot, span)] = e.reshape(span, tile, tile)
            dp_scr[pl.ds(slot, span)] = dp.reshape(span, tile, tile)
            tops[slot] = new
            top[...] = new
            total[...] = total[...] * shrink + jnp.sum(e, axis=0, keepdims=True)
            delta[...] = delta[...] * shrink + jnp.sum(e * dp, axis=0, keepdims=True)

        def grads(slot, row, time, span):
            for step in range(span):

                @pl.when(jnp.logical_or(qt == 0, jnp.logical_not(seen(0, row, time + step))))
                def _():
                    acc[:, row, time + step] = jnp.zeros((2,) + acc.shape[3:], jnp.float32)

            def flat(ref):
                return ref[pl.ds(slot, span)].reshape(span * tile, tile)

            times = pl.ds(time, span)
            shape = (span, tile, HD)
            p = flat(e_scr) * (jnp.exp2((tops[slot] - top[...]) * (SCALE * LOG2E)) * total[...])
            ds = (p * (flat(dp_scr) - delta[...])).astype(jnp.bfloat16)
            acc[1, row, times] += dot(p.astype(jnp.bfloat16), g, ((1,), (0,))).reshape(shape)
            acc[0, row, times] += dot(ds, q, ((1,), (0,))).reshape(shape)
            dqt[...] += dot(near(0, row, time, span), ds, ((0,), (0,)))

        over_visible(scores)
        total[...] = 1.0 / total[...]
        delta[...] = delta[...] * total[...]
        over_visible(grads)
        dq_ref[0, rows, :] = (dqt[...] * SCALE).T.astype(jnp.bfloat16)
        return carry

    lax.fori_loop(0, 2, one_tile, 0)

    def hand_out(index, carry):
        row, time = lax.div(index, 4), lax.rem(index, 4)
        used = jnp.logical_or(seen(0, row, time), seen(1, row, time))

        @pl.when(used)
        def _():
            dkv_ref[0, 0, row, time] = (acc[0, row, time] * SCALE).astype(jnp.bfloat16)
            dkv_ref[0, 1, row, time] = acc[1, row, time].astype(jnp.bfloat16)

        @pl.when(jnp.logical_not(used))
        def _():
            dkv_ref[0, :, row, time] = jnp.zeros((2,) + acc.shape[3:], jnp.bfloat16)

        return carry

    lax.fori_loop(0, 12, hand_out, 0)


def attend(vis, q, g, kv):
    heads, rows, _ = q.shape
    tile = rows // 2
    by_head = lambda shape: pl.BlockSpec(
        (1,) + shape, lambda n, vis: (n,) + (0,) * len(shape)
    )
    pairs = heads * 18
    return pl.pallas_call(
        attend_kernel,
        grid_spec=pltpu.PrefetchScalarGridSpec(
            num_scalar_prefetch=1,
            grid=(heads,),
            in_specs=[
                by_head((rows, HD)),
                by_head((rows, HD)),
                by_head((2, 3, 4, tile, HD)),
            ],
            out_specs=[by_head((rows, HD)), by_head((2, 3, 4, tile, HD))],
            scratch_shapes=[
                pltpu.VMEM((9, tile, tile), jnp.float32),
                pltpu.VMEM((9, tile, tile), jnp.float32),
                pltpu.VMEM((2, 3, 4, tile, HD), jnp.float32),
                pltpu.VMEM((HD, tile), jnp.float32),
                pltpu.VMEM((9, 1, tile), jnp.float32),
                pltpu.VMEM((1, tile), jnp.float32),
                pltpu.VMEM((1, tile), jnp.float32),
                pltpu.VMEM((1, tile), jnp.float32),
            ],
        ),
        out_shape=[
            jax.ShapeDtypeStruct(q.shape, jnp.bfloat16),
            jax.ShapeDtypeStruct(kv.shape, jnp.bfloat16),
        ],
        compiler_params=pltpu.CompilerParams(
            dimension_semantics=("arbitrary",), vmem_limit_bytes=48 * 2**20
        ),
        cost_estimate=pl.CostEstimate(
            flops=pairs * 5 * tile * tile * HD,
            bytes_accessed=4 * kv.size + 6 * q.size,
            transcendentals=pairs * tile * tile // 2,
        ),
        name="attend",
    )(vis, q, g, kv)


def neighbours():
    seq = lax.axis_index("seq")
    row, slab = lax.rem(seq, GH), lax.div(seq, GH)
    slabs = lax.axis_size("seq") // GH
    return (
        (row > 0, seq - 1),
        (row < GH - 1, seq + 1),
        (slab > 0, seq - GH),
        (slab < slabs - 1, seq + GH),
    )


def far_row():
    row = lax.rem(lax.axis_index("seq"), GH)
    odd = lax.rem(row, 2)
    exists = jnp.where(odd == 1, row < GH - 1, row > 0)
    return exists, 2 * odd


def greet(partners, peers):
    barrier = pltpu.get_barrier_semaphore()
    for peer in peers:
        pl.semaphore_signal(barrier, inc=1, device_id={"head": peer}, device_id_type=MESH)
    for exists, seq in partners:

        @pl.when(exists)
        def _():
            pl.semaphore_signal(barrier, inc=1, device_id={"seq": seq}, device_id_type=MESH)

    count = sum(exists.astype(jnp.int32) for exists, _ in partners)
    pl.semaphore_wait(barrier, count + len(peers))


def remote(src, dst, sems, index, device):
    return pltpu.make_async_remote_copy(
        src_ref=src,
        dst_ref=dst,
        send_sem=sems[0].at[index],
        recv_sem=sems[1].at[index],
        device_id=device,
        device_id_type=MESH,
    )


def for_heads(heads, body):
    def step(n, carry):
        body(n)
        return carry

    lax.fori_loop(0, heads, step, 0)


def gather_kernel(
    nh, q_in, k_in, v_in, g_in, q_out, g_out, kv_out, stage_buf, load, own, swap_s, swap_r, near_s, near_r
):
    heads, _, _, _, tile, _ = kv_out.shape
    rows = q_in.shape[0]
    h = lax.axis_index("head")
    partners = neighbours()
    up, down, before, after = partners
    peers = [lax.rem(h + j, nh) for j in range(1, nh)]
    senders = [lax.rem(h + nh - j, nh) for j in range(1, nh)]
    sources = (k_in, v_in, q_in, g_in)
    far_exists, far = far_row()
    share = nh // 2

    def place(array, n, owner):
        if array < 2:
            offset = pl.multiple_of(lax.rem(owner, share) * rows, rows)
            return kv_out.at[n, array, 1, 1 + lax.div(owner, share), pl.ds(offset, rows)]
        out = q_out if array == 2 else g_out
        return out.at[n, pl.ds(pl.multiple_of(owner * rows, rows), rows)]

    def columns(array, n, owner):
        start = pl.multiple_of((owner * heads + n) * HD, HD)
        return sources[array].at[:, pl.ds(start, HD)]

    def staged(array, n, owner):
        return stage_buf.at[array, owner * heads + n]

    def loaded(array, n, owner):
        return pltpu.make_async_copy(
            columns(array, n, owner), staged(array, n, owner), load.at[array, owner * heads + n]
        )

    def kept(array, n):
        return pltpu.make_async_copy(staged(array, n, h), place(array, n, h), own.at[array, n])

    def swapped(array, n, j, owner):
        return remote(
            staged(array, n, peers[j]),
            place(array, n, owner),
            (swap_s, swap_r),
            (array, j, n),
            {"head": peers[j]},
        )

    def start_load(arrays, n):
        for array in arrays:
            for owner in peers + [h]:
                loaded(array, n, owner).start()

    def start_swap(arrays, n):
        for array in arrays:
            for j in range(nh - 1):
                loaded(array, n, peers[j]).wait()
                swapped(array, n, j, h).start()
            loaded(array, n, h).wait()
            kept(array, n).start()

    def wait_swap(arrays, n):
        for array in arrays:
            for j in range(nh - 1):
                swapped(array, n, j, senders[j]).wait_recv()
            kept(array, n).wait()

    def block(n, row, first, count):
        return kv_out.at[n, :, row, pl.ds(first, count)]

    def copies(kind, n):
        if kind == 0:
            mine, plan = (1, 1, 2), ((up, (2, 1, 2), (0, 1, 2)), (down, (0, 1, 2), (2, 1, 2)))
        elif kind == 1:
            plan = ((before, (1, 3, 1), (1, 0, 1)), (after, (1, 0, 1), (1, 3, 1)))
        else:
            time = 0 if kind == 2 else 3
            plan = ((up, (2, time, 1), (0, time, 1)), (down, (0, time, 1), (2, time, 1)))
        found = []
        for side, (partner, there, here) in enumerate(plan):
            exists = partner[0]
            if kind == 2:
                exists = jnp.logical_and(exists, far != 2 * side)
            if kind == 1:
                mine = (1, 1 + side, 1)
            elif kind > 1:
                mine = (1, time, 1)
            device = {"seq": partner[1]}
            send = functools.partial(
                remote,
                block(n, *mine), block(n, *there), (near_s, near_r), (kind, side, n), device
            )
            arrive = functools.partial(
                remote,
                block(n, *mine), block(n, *here), (near_s, near_r), (kind, 1 - side, n), device
            )
            found.append((exists, send, arrive))
        return found

    def diagonal(n):
        device = {"seq": after[1]}
        return remote(
            block(n, far, 2, 1), block(n, far, 0, 1), (near_s, near_r), (4, 0, n), device
        )

    sends_diagonal = jnp.logical_and(after[0], far_exists)
    gets_diagonal = jnp.logical_and(before[0], far_exists)

    def each(kind, n, act):
        for exists, send, arrive in copies(kind, n):

            @pl.when(exists)
            def _():
                act(send, arrive)

    def start(send, arrive):
        send().start()

    for_heads(heads, lambda n: start_load((0, 1), n))
    for_heads(heads, lambda n: start_load((2, 3), n))
    greet(partners, peers)
    ahead = min(3, heads)
    for_heads(ahead, lambda n: start_swap((0, 1), n))

    def forward(n):
        each(0, n, lambda send, arrive: arrive().wait_recv())

        @pl.when(sends_diagonal)
        def _():
            diagonal(n).start()

        for exists_side, kind in ((0, 2), (1, 3)):
            exists, _, arrive = copies(1, n)[exists_side]

            @pl.when(exists)
            def _():
                arrive().wait_recv()
                each(kind, n, start)

    def stage(n):
        wait_swap((0, 1), n)
        each(0, n, start)
        each(1, n, start)

        @pl.when(n + ahead < heads)
        def _():
            start_swap((0, 1), n + ahead)

        @pl.when(n + ahead >= heads)
        def _():
            start_swap((2, 3), n + ahead - heads)

        @pl.when(n >= lag)
        def _():
            forward(n - lag)

    lag = min(2, heads)
    for_heads(heads, stage)
    for_heads(heads - ahead, lambda n: start_swap((2, 3), ahead + n))
    for_heads(lag, lambda n: forward(heads - lag + n))

    def finish(n):
        wait_swap((2, 3), n)
        for array in range(4):
            for j in range(nh - 1):
                swapped(array, n, j, h).wait_send()
        each(0, n, lambda send, arrive: send().wait_send())
        each(1, n, lambda send, arrive: send().wait_send())

        @pl.when(sends_diagonal)
        def _():
            diagonal(n).wait_send()

        @pl.when(gets_diagonal)
        def _():
            diagonal(n).wait_recv()

        for partner, kind in ((before, 2), (after, 3)):

            @pl.when(partner[0])
            def _():
                each(kind, n, lambda send, arrive: (send().wait_send(), arrive().wait_recv()))

    for_heads(heads, finish)


def exchange_in(queries, keys, values, out_grad):
    nh = lax.axis_size("head")
    rows, width = queries.shape
    heads, tile = width // HD // nh, rows * nh // 2
    dma = pltpu.SemaphoreType.DMA
    return pl.pallas_call(
        functools.partial(gather_kernel, nh),
        in_specs=[pl.BlockSpec(memory_space=pl.ANY)] * 4,
        out_specs=[pl.BlockSpec(memory_space=pl.ANY)] * 3,
        out_shape=[
            jax.ShapeDtypeStruct((heads, 2 * tile, HD), jnp.bfloat16),
            jax.ShapeDtypeStruct((heads, 2 * tile, HD), jnp.bfloat16),
            jax.ShapeDtypeStruct((heads, 2, 3, 4, tile, HD), jnp.bfloat16),
        ],
        scratch_shapes=[
            pltpu.VMEM((4, nh * heads, rows, HD), jnp.bfloat16),
            dma((4, nh * heads)),
            dma((4, heads)),
            dma((4, nh - 1, heads)),
            dma((4, nh - 1, heads)),
            dma((5, 2, heads)),
            dma((5, 2, heads)),
        ],
        compiler_params=pltpu.CompilerParams(
            collective_id=0, has_side_effects=True, vmem_limit_bytes=44 * 2**20
        ),
        name="gather",
    )(queries, keys, values, out_grad)


def scatter_kernel(
    nh,
    dq_in,
    dkv_in,
    dq_out,
    dk_out,
    dv_out,
    mine,
    sides,
    edges,
    times,
    final,
    landed,
    crossed,
    merged,
    load,
    load_far,
    pull,
    push,
    swap_s,
    swap_r,
    near_s,
    near_r,
):
    heads, _, _, _, tile, _ = dkv_in.shape
    rows = dq_out.shape[0]
    h = lax.axis_index("head")
    partners = neighbours()
    up, down, before, after = partners
    peers = [lax.rem(h + j, nh) for j in range(1, nh)]
    senders = [lax.rem(h + nh - j, nh) for j in range(1, nh)]
    outs = (dk_out, dv_out, dq_out)
    far_exists, far = far_row()
    far_side = lax.div(far, 2)
    sends_cross = jnp.logical_and(before[0], far_exists)
    gets_cross = jnp.logical_and(after[0], far_exists)

    def part(array, n, owner):
        span = pl.ds(pl.multiple_of(owner * rows, rows), rows)
        return dq_in.at[n, span] if array == 2 else final.at[n, array, span]

    def columns(array, n, owner):
        start = pl.multiple_of((owner * heads + n) * HD, HD)
        return outs[array].at[:, pl.ds(start, HD)]

    def pulled(n):
        return pltpu.make_async_copy(part(2, n, h), landed.at[2, h * heads + n], pull.at[n])

    def stored(array, n, owner):
        place = owner * heads + n
        src = landed.at[array, place]
        if array < 2 and owner is h:
            src = part(array, n, h)
        return pltpu.make_async_copy(src, columns(array, n, owner), push.at[array, place])

    def swapped(array, n, j, owner):
        return remote(
            part(array, n, peers[j]),
            landed.at[array, owner * heads + n],
            (swap_s, swap_r),
            (array, j, n),
            {"head": peers[j]},
        )

    def start_swap(arrays, n):
        for array in arrays:
            for j in range(nh - 1):
                swapped(array, n, j, h).start()
            if array == 2:
                pulled(n).start()
            else:
                stored(array, n, h).start()

    def settle(arrays, n):
        for array in arrays:
            if array == 2:
                pulled(n).wait()
                stored(array, n, h).start()
            for j in range(nh - 1):
                swapped(array, n, j, senders[j]).wait_recv()
                stored(array, n, senders[j]).start()

    def copies(kind, n):
        if kind == 0:
            plan = ((up, 0), (down, 1))
        else:
            plan = ((before, 0), (after, 1))
        found = []
        for partner, side in plan:
            exists = partner[0]
            if kind == 0:
                exists = jnp.logical_and(exists, far_side != side)
                src, dst, here = dkv_in.at[n, :, 2 * side], sides.at[n, 1 - side], sides.at[n, side]
            else:
                src, dst, here = edges.at[n, side], times.at[n, 1 - side], times.at[n, side]
            device = {"seq": partner[1]}
            send = functools.partial(
                remote, src, dst, (near_s, near_r), (kind, side, n), device)
            arrive = functools.partial(
                remote, src, here, (near_s, near_r), (kind, 1 - side, n), device)
            found.append((exists, send, arrive))
        return found

    def each(kind, n, act):
        for exists, send, arrive in copies(kind, n):

            @pl.when(exists)
            def _():
                act(send, arrive)

    def loaded(n):
        return pltpu.make_async_copy(dkv_in.at[n, :, 1], mine.at[n], load.at[n])

    def loaded_far(n):
        return pltpu.make_async_copy(dkv_in.at[n, :, far, 2], merged.at[n], load_far.at[n])

    def across(n, k, side):
        time = (1, 3, 2)[k]
        src = merged.at[n] if k == 2 else dkv_in.at[n, :, far, time]
        device = {"seq": lax.axis_index("seq") + far - 1}
        index = (2 + k // 2, k % 2, n)
        return remote(src, sides.at[n, side, :, time], (near_s, near_r), index, device)

    def cross(n):
        device = {"seq": before[1]}
        return remote(
            dkv_in.at[n, :, far, 0], crossed.at[n], (near_s, near_r), (3, 1, n), device
        )

    greet(partners, peers)

    def begin(n):
        @pl.when(sends_cross)
        def _():
            cross(n).start()

        each(0, n, lambda send, arrive: send().start())
        loaded(n).start()

        @pl.when(far_exists)
        def _():
            loaded_far(n).start()
            across(n, 0, 1 - far_side).start()
            across(n, 1, 1 - far_side).start()

    def merge(n):
        @pl.when(far_exists)
        def _():
            loaded_far(n).wait()

        @pl.when(gets_cross)
        def _():
            cross(n).wait_recv()
            total = merged[n].astype(jnp.float32) + crossed[n].astype(jnp.float32)
            merged[n] = total.astype(jnp.bfloat16)

        @pl.when(far_exists)
        def _():
            across(n, 2, 1 - far_side).start()

    ahead = min(4, heads)
    for_heads(ahead, begin)
    for_heads(heads, lambda n: start_swap((2,), n))
    for buffer, pair in ((sides, (up, down)), (times, (before, after))):
        for side, partner in enumerate(pair):

            @pl.when(jnp.logical_not(partner[0]))
            def _():
                def clear(n):
                    buffer[n, side] = jnp.zeros(buffer.shape[2:], buffer.dtype)

                for_heads(heads, clear)

    def clear_far(n):
        sides[n, far_side, :, 0] = jnp.zeros(merged.shape[1:], merged.dtype)

    for_heads(heads, clear_far)

    def column(n, which, time):
        terms = (mine[n, which, time], sides[n, 0, which, time], sides[n, 1, which, time])
        first, second, third = (term.astype(jnp.float32) for term in terms)
        return first + second + third

    def wrap_up(n):
        each(1, n, lambda send, arrive: arrive().wait_recv())
        for which in range(2):
            for place in range(2):
                total = column(n, which, 1 + place) + times[n, place, which].astype(jnp.float32)
                final[n, which, pl.ds(place * tile, tile)] = total.astype(jnp.bfloat16)
        start_swap((0, 1), n)
        settle((2,), n)

        @pl.when(n >= lag)
        def _():
            settle((0, 1), n - lag)

    lag = min(2, heads)

    def stage(n):
        each(0, n, lambda send, arrive: arrive().wait_recv())
        loaded(n).wait()

        @pl.when(far_exists)
        def _():
            for k in range(3):
                across(n, k, far_side).wait_recv()

        for which in range(2):
            for side in range(2):
                edges[n, side, which] = column(n, which, 3 * side).astype(jnp.bfloat16)
        each(1, n, lambda send, arrive: send().start())

    def step(n):
        merge(n)

        @pl.when(n + ahead < heads)
        def _():
            begin(n + ahead)

        @pl.when(n >= 1)
        def _():
            stage(n - 1)

        @pl.when(n >= 2)
        def _():
            wrap_up(n - 2)

    for_heads(heads, step)
    stage(heads - 1)
    for_heads(lag, lambda n: wrap_up(heads - lag + n))
    for_heads(lag, lambda n: settle((0, 1), heads - lag + n))

    def finish(n):
        for array in range(3):
            for j in range(nh - 1):
                swapped(array, n, j, h).wait_send()
                stored(array, n, senders[j]).wait()
            stored(array, n, h).wait()
        each(0, n, lambda send, arrive: send().wait_send())
        each(1, n, lambda send, arrive: send().wait_send())

        @pl.when(sends_cross)
        def _():
            cross(n).wait_send()

        @pl.when(far_exists)
        def _():
            for k in range(3):
                across(n, k, 1 - far_side).wait_send()

    for_heads(heads, finish)


def exchange_out(dq, dkv):
    nh = lax.axis_size("head")
    heads, rows, _ = dq.shape
    tile = rows // 2
    dma = pltpu.SemaphoreType.DMA
    whole = jax.ShapeDtypeStruct((rows // nh, nh * heads * HD), jnp.bfloat16)

    def held(*shape):
        return pltpu.VMEM(shape + (HD,), jnp.bfloat16)

    return pl.pallas_call(
        functools.partial(scatter_kernel, nh),
        in_specs=[pl.BlockSpec(memory_space=pl.ANY)] * 2,
        out_specs=[pl.BlockSpec(memory_space=pl.ANY)] * 3,
        out_shape=[whole] * 3,
        scratch_shapes=[
            held(heads, 2, 4, tile),
            held(heads, 2, 2, 4, tile),
            held(heads, 2, 2, tile),
            held(heads, 2, 2, tile),
            held(heads, 2, 2 * tile),
            held(3, nh * heads, rows // nh),
            held(heads, 2, tile),
            held(heads, 2, tile),
            dma((heads,)),
            dma((heads,)),
            dma((heads,)),
            dma((3, nh * heads)),
            dma((3, nh - 1, heads)),
            dma((3, nh - 1, heads)),
            dma((4, 2, heads)),
            dma((4, 2, heads)),
        ],
        compiler_params=pltpu.CompilerParams(
            collective_id=1, has_side_effects=True, vmem_limit_bytes=44 * 2**20
        ),
        name="scatter",
    )(dq, dkv)


def per_device(queries, keys, values, out_grad, window):
    q, g, kv = exchange_in(queries, keys, values, out_grad)
    dq, dkv = attend(visible_slots(window, q.shape[0]), q, g, kv)
    return exchange_out(dq, dkv)


def solution(mesh):
    rows = P(("seq", "head"), None)
    return jax.shard_map(
        per_device,
        mesh=mesh,
        in_specs=(rows, rows, rows, rows, P()),
        out_specs=(rows, rows, rows),
        check_vma=False,
    )
```
